512 devices in a mesh: req: 32 (over x, y, core), tp: 16 (over z).
Axes of the slice: x: 4, y: 4, z: 16, core: 2. Of those that a mesh axis runs over, the one named last changes fastest.
Arguments:
- queries: bfloat16 [64, 8192], P('req'), may hold values from -8 to 8
- image_cache: bfloat16 [32, 1664, 2048], P('req', 'tp'), may hold values from -12 to 12
- image_lists: int32 [64, 4], replicated, may hold values from 0 to 31, as said below
- cited_count: int32 [64], replicated, may hold values from 1 to 4, as said below
- image_slot: int32 [32], replicated, may hold values from 0 to 31, as said below
Outputs:
- attended: float32 [64, 8192], P('req', 'tp')
The draws below stay inside these ranges and needn't reach their ends.
Inputs may be any that keep to these rules, and one draw needn't show every extreme that they name: `image_lists`: the 4 image ids of a row are different; entry 0 of request r names an image whose storage slot is held by the index of req before that of request r (counted round). `cited_count`: some request cites 4 images and some request one. `image_slot`: every slot holds exactly one image.
All inputs are finite; a program needn't handle non-finite values.
Results may differ from the reference program's by a relative error of at most 0.0007.
Values may be sent and summed in bfloat16 or wider, within the bound.
A program may use at most 128 MiB of HBM per device.

```python
import math
import jax
import jax.numpy as jnp
from jax import lax

HEADS = 64
KVH = 8
HD = 128
LISTS = 4
IMG_TOK = 1601
IMG_SLOTS = 1664
R_DEV = 2
IMG_DEV = 1
REQS = 64
IMAGES = 32


def slot_order(key):
    order_key = jax.random.fold_in(key, 57)
    return jax.random.permutation(order_key, IMAGES).astype(jnp.int32)


def draw_queries(key, part):
    key = jax.random.fold_in(key, 1)
    key_drawn = jax.random.fold_in(key, 0)
    drawn = jnp.clip(2.5 * jax.random.normal(key_drawn, (REQS, HEADS * HD), jnp.float32), -8.0, 8.0)
    return drawn.astype(jnp.bfloat16)


def draw_image_cache(key, part):
    key = jax.random.fold_in(key, 2)
    width = KVH * HD
    base = jnp.clip(jax.random.normal(key, (IMAGES, IMG_SLOTS, 2 * width), jnp.float32), -6.0, 6.0)
    return base.astype(jnp.bfloat16)


def draw_image_slot(key, part):
    return slot_order(key)


def draw_image_lists(key, part):
    order = slot_order(key)
    key = jax.random.fold_in(key, 4)
    key_first, key_rest = jax.random.split(key, 2)
    holders = IMAGES // IMG_DEV
    request_ids = jnp.arange(REQS, dtype=jnp.int32)
    owner = request_ids // R_DEV
    first = (owner - 1) % holders * IMG_DEV + jax.random.randint(key_first, (REQS,), 0, IMG_DEV)
    row_keys = jax.random.split(key_rest, REQS)
    offsets = jax.vmap(lambda row_key: jax.random.permutation(row_key, IMAGES - 1)[:LISTS - 1] + 1)(row_keys)
    offsets = jnp.concatenate([jnp.zeros((REQS, 1), jnp.int32), offsets.astype(jnp.int32)], axis=1)
    slots = (first[:, None] + offsets) % IMAGES
    ids_of_slot = jnp.zeros((IMAGES,), jnp.int32).at[order].set(jnp.arange(IMAGES, dtype=jnp.int32))
    return ids_of_slot[slots].astype(jnp.int32)


def draw_cited_count(key, part):
    key = jax.random.fold_in(key, 3)
    key_base, key_high, key_step = jax.random.split(key, 3)
    counts = jax.random.randint(key_base, (REQS,), 1, LISTS + 1)
    highest = jax.random.randint(key_high, (), 0, REQS)
    lowest = (highest + jax.random.randint(key_step, (), 1, REQS)) % REQS
    request_ids = jnp.arange(REQS, dtype=jnp.int32)
    counts = jnp.where(request_ids == highest, LISTS, counts)
    counts = jnp.where(request_ids == lowest, 1, counts)
    return counts.astype(jnp.int32)


def setup_inputs(seed: int = 0) -> dict:
    streams_of = jax.random.split(jax.random.key(seed), 6)
    queries = draw_queries(jax.random.fold_in(streams_of[5], 71), 0)
    image_cache = draw_image_cache(jax.random.fold_in(streams_of[5], 71), 0)
    image_lists = draw_image_lists(jax.random.fold_in(streams_of[5], 71), 0)
    cited_count = draw_cited_count(jax.random.fold_in(streams_of[5], 71), 0)
    image_slot = draw_image_slot(jax.random.fold_in(streams_of[5], 71), 0)
    return dict(queries=queries, image_cache=image_cache, image_lists=image_lists, cited_count=cited_count, image_slot=image_slot)


negative_floor = -1e+30

def reference(queries, image_cache, image_lists, cited_count, image_slot):
    scale = 1.0 / math.sqrt(HD)
    token_ok = jnp.arange(IMG_SLOTS, dtype=jnp.int32) < IMG_TOK

    def one_request(packed):
        query_row, listed_images, count_here = packed
        slots = image_slot[listed_images].astype(jnp.int32)
        blocks = jnp.take(image_cache, slots, axis=0).astype(jnp.float32)
        keys = blocks[:, :, :KVH * HD].reshape(LISTS, IMG_SLOTS, KVH, HD)
        values = blocks[:, :, KVH * HD:].reshape(LISTS, IMG_SLOTS, KVH, HD)
        grouped = query_row.astype(jnp.float32).reshape(KVH, HEADS // KVH, HD)
        scores = jnp.einsum('kgd,jskd->kgjs', grouped, keys, precision=lax.Precision.HIGHEST) * scale
        allowed = (jnp.arange(LISTS, dtype=jnp.int32) < count_here)[:, None] & token_ok[None, :]
        scores = jnp.where(allowed[None, None], scores, negative_floor)
        peak = lax.optimization_barrier(jnp.max(scores, axis=(2, 3)))
        weights = jnp.where(allowed[None, None], jnp.exp(scores - peak[:, :, None, None]), 0.0)
        totals = lax.optimization_barrier(jnp.sum(weights, axis=(2, 3)))
        weighted = jnp.einsum('kgjs,jskd->kgd', weights, values, precision=lax.Precision.HIGHEST)
        return (weighted / totals[:, :, None]).reshape(HEADS * HD).astype(jnp.float32)
    return lax.map(one_request, (queries, image_lists, cited_count))
```

```python
import functools
import math

import jax
import jax.numpy as jnp
from jax import lax
from jax.experimental import pallas as pl
from jax.experimental.pallas import tpu as pltpu
from jax.sharding import PartitionSpec as P

KVH = 8
GROUP = 8
HD = 128
IMG_TOK = 1601
LISTS = 4
NX = 4
NY = 4
NZ = 16
CHIPS = NX * NY
TOK = 104
TOK_SENT = 112
SEG = 128
SEGS = 4
KV_HERE = KVH // 2
ROWS = 16
BLOCK = KV_HERE * ROWS
NEG = -1e30
SCALE = math.log2(math.e) / math.sqrt(HD)
MESH = pl.DeviceIdType.MESH
OFFSETS = sorted(
    ((i, j) for i in range(NX) for j in range(NY) if (i, j) != (0, 0)),
    key=lambda o: -(min(o[0], NX - o[0]) + min(o[1], NY - o[1])),
)
NEAR = tuple(d for d in range(-4, 5) if d)


def wait_bytes(ref, sem):
    pltpu.make_async_copy(ref, ref, sem).wait()


def kernel(
    q_ref, cache_ref, lists_ref, count_ref, slot_ref, out_ref,
    qbuf, kbuf, vbuf, ksend, vsend, bias, obuf, rbuf, zsend, zbuf,
    g_send, g_recv, kv_send, kv_recv, r_send, r_recv, z_send, z_recv, z_ready,
):
    req = lax.axis_index("req")
    z = lax.axis_index("tp")
    chip = lax.div(req, 2)
    core = lax.rem(req, 2)
    x = lax.div(chip, NY)
    y = lax.rem(chip, NY)
    par = lax.rem(z, 2)

    def device(x_, y_, c_, z_):
        return ((x_ * NY + y_) * 2 + c_, z_)

    def moved(dx, dy):
        return lax.rem(x + dx, NX), lax.rem(y + dy, NY)

    other_core = device(x, y, 1 - core, z)
    other_slice = device(x, y, core, z + 1 - 2 * par)

    barrier = pltpu.get_barrier_semaphore()
    met = [other_core]
    met += [device(*moved(dx, dy), core, z) for dx, dy in OFFSETS]
    met += [device(x, y, core, lax.rem(z + d + NZ, NZ)) for d in NEAR]
    for there in met:
        pl.semaphore_signal(barrier, inc=1, device_id=there, device_id_type=MESH)

    half = KV_HERE * GROUP * HD
    own = q_ref[:, pl.ds(pl.multiple_of(par * half, half), half)].astype(jnp.float32)
    for k in range(KV_HERE):
        rows = [
            own[r : r + 1, (k * GROUP + g) * HD : (k * GROUP + g + 1) * HD]
            for r in range(2)
            for g in range(GROUP)
        ]
        qbuf[chip, k * ROWS : (k + 1) * ROWS, :] = jnp.concatenate(rows, axis=0).astype(jnp.bfloat16)

    zeros = jnp.zeros((32, HD), jnp.bfloat16)
    for s in range(SEGS):
        for k in range(KV_HERE):
            kbuf[s, k, TOK_SENT:, :] = zeros[: SEG - TOK_SENT]
            vbuf[s, k, TOK_SENT:, :] = zeros[: SEG - TOK_SENT]
    tail = jnp.zeros((TOK_SENT - TOK, HD), jnp.bfloat16)
    for k in range(KV_HERE):
        for buf, base in ((kbuf, 0), (vbuf, KVH * HD)):
            at = pl.multiple_of(base + (par * KV_HERE + k) * HD, HD)
            part = cache_ref[0, :, pl.ds(at, HD)]
            buf[0, k, :TOK_SENT, :] = jnp.concatenate([part, tail], axis=0)
        for buf, base in ((ksend, 0), (vsend, KVH * HD)):
            at = pl.multiple_of(base + ((1 - par) * KV_HERE + k) * HD, HD)
            part = cache_ref[0, :, pl.ds(at, HD)]
            buf[k] = jnp.concatenate([part, tail], axis=0)

    pl.semaphore_wait(barrier, len(met))
    for d in (-4, 4):
        there = device(x, y, core, lax.rem(z + d + NZ, NZ))
        pl.semaphore_signal(z_ready, inc=1, device_id=there, device_id_type=MESH)

    def remote(src, dst, send, recv, there):
        return pltpu.make_async_remote_copy(
            src_ref=src, dst_ref=dst, send_sem=send, recv_sem=recv,
            device_id=there, device_id_type=MESH,
        )

    sent = pl.ds(0, TOK_SENT)
    to_slice = [
        remote(buf, dst.at[2, :, sent], kv_send.at[i], kv_recv.at[i], other_slice)
        for i, (buf, dst) in enumerate(((ksend, kbuf), (vsend, vbuf)))
    ]
    to_core = [
        remote(buf.at[0, :, sent], buf.at[1, :, sent], kv_send.at[2 + i], kv_recv.at[2 + i], other_core)
        for i, buf in enumerate((kbuf, vbuf))
    ]
    onward = [
        remote(buf.at[2, :, sent], buf.at[3, :, sent], kv_send.at[4 + i], kv_recv.at[4 + i], other_core)
        for i, buf in enumerate((kbuf, vbuf))
    ]

    to_slice[0].start()
    for dx, dy in OFFSETS:
        remote(qbuf.at[chip], qbuf.at[chip], g_send, g_recv, device(*moved(dx, dy), core, z)).start()
    to_slice[1].start()
    to_core[0].start()
    to_core[1].start()

    lanes = lax.broadcasted_iota(jnp.int32, (GROUP, SEG), 1)
    seen = []
    for slice_ in (z, z + 1 - 2 * par):
        ok = (lanes < TOK) & (slice_ * TOK + lanes < IMG_TOK)
        seen.append(jnp.where(ok, 0.0, NEG))

    @pl.loop(0, CHIPS)
    def _(d):
        for r in range(2):
            request = 4 * d + 2 * core + r
            cited = count_ref[request]
            hit = [jnp.int32(0), jnp.int32(0)]
            for j in range(LISTS):
                slot = slot_ref[lists_ref[request, j]]
                here = jnp.where(j < cited, 1, 0)
                for i, held in enumerate((req, 2 * chip + 1 - core)):
                    hit[i] = hit[i] + jnp.where(slot == held, here, 0)
            for i in range(2):
                level = jnp.where(hit[i] > 0, 0.0, NEG)
                for s in range(2):
                    at = (2 * s + i) * SEG
                    bias[d, r * GROUP : (r + 1) * GROUP, at : at + SEG] = seen[s] + level

    to_slice[0].wait_recv()
    onward[0].start()
    to_slice[1].wait_recv()
    onward[1].start()
    wait_bytes(qbuf.at[pl.ds(0, CHIPS - 1)], g_recv)
    to_core[0].wait_recv()
    to_core[1].wait_recv()
    onward[0].wait_recv()
    onward[1].wait_recv()

    every = CHIPS * ROWS
    lane = lax.broadcasted_iota(jnp.int32, (CHIPS, GROUP, HD), 2)
    stat = jnp.zeros((CHIPS, GROUP, HD), jnp.float32)
    allowed = bias[...].reshape(every, SEGS * SEG)
    for k in range(KV_HERE):
        at = slice(k * ROWS, (k + 1) * ROWS)
        queries = qbuf[:, at, :].reshape(every, HD)
        keys = kbuf[:, k].reshape(SEGS * SEG, HD)
        values = vbuf[:, k].reshape(SEGS * SEG, HD)
        scores = lax.dot_general(
            queries, keys, (((1,), (1,)), ((), ())), preferred_element_type=jnp.float32
        )
        scores = scores * SCALE + allowed
        peak = jnp.max(scores, axis=1, keepdims=True)
        weights = jnp.exp2(scores - peak)
        total = jnp.sum(weights, axis=1, keepdims=True)
        high = weights.astype(jnp.bfloat16)
        low = (weights - high.astype(jnp.float32)).astype(jnp.bfloat16)
        weighted = jnp.dot(high, values, preferred_element_type=jnp.float32)
        weighted += jnp.dot(low, values, preferred_element_type=jnp.float32)
        obuf[:, at, :] = (weighted / total).reshape(CHIPS, ROWS, HD)
        size = (peak + jnp.log2(total)).reshape(CHIPS, 2, GROUP, 1)
        for r in range(2):
            stat = jnp.where(lane == r * KV_HERE + k, size[:, r], stat)
    obuf[:, BLOCK:, :] = stat

    for dx, dy in OFFSETS:
        x_, y_ = moved(dx, dy)
        remote(obuf.at[x_ * NY + y_], rbuf.at[chip], r_send, r_recv, device(x_, y_, core, z)).start()
    rbuf[chip] = obuf[chip]
    wait_bytes(rbuf.at[pl.ds(0, CHIPS - 1)], r_recv)

    sizes = rbuf[:, BLOCK:, :]
    largest = jnp.max(sizes, axis=0)
    share = jnp.exp2(sizes - largest[None])
    total = jnp.sum(share, axis=0)
    share = share / total[None]
    size = largest + jnp.log2(total)
    low_rows = lax.broadcasted_iota(jnp.int32, (GROUP, HD), 0) < GROUP // 2
    pl.semaphore_wait(z_ready, 2)
    for k in range(KV_HERE):
        both, logs = [], []
        for r in range(2):
            at = k * ROWS + r * GROUP
            col = r * KV_HERE + k
            part = jnp.zeros((GROUP, HD), jnp.float32)
            for s in range(CHIPS):
                part += rbuf[s, at : at + GROUP, :] * share[s, :, col : col + 1]
            both.append(part)
            logs.append(jnp.broadcast_to(size[:, col : col + 1], (GROUP, HD)))
        for h in range(2):
            for row, (a, b) in ((0, both), (GROUP, logs)):
                if h == 0:
                    tile = jnp.where(low_rows, a, pltpu.roll(b, GROUP // 2, 0))
                else:
                    tile = jnp.where(low_rows, pltpu.roll(a, GROUP // 2, 0), b)
                zsend[2 * k + h, row : row + GROUP, :] = tile
            there = 2 * (par * KV_HERE + k) + h

            @pl.when(there != z)
            def _(k=k, h=h, there=there):
                remote(
                    zsend.at[2 * k + h], zbuf.at[lax.div(z, 2)], z_send.at[2 * k + h],
                    z_recv.at[lax.div(z, 2)], device(x, y, core, there),
                ).start()

            @pl.when(there == z)
            def _(k=k, h=h):
                zbuf[lax.div(z, 2)] = zsend[2 * k + h]

    theirs = lax.div(z, NZ // 2)
    for i in range(NZ // 2):

        @pl.when(2 * i + theirs != z)
        def _(i=i):
            wait_bytes(zbuf.at[i], z_recv.at[i])

    sizes = zbuf[:, GROUP:, :]
    largest = jnp.max(sizes, axis=0)
    share = jnp.exp2(sizes - largest[None])
    out_ref[...] = jnp.sum(zbuf[:, :GROUP, :] * share, axis=0) / jnp.sum(share, axis=0)

    wait_bytes(qbuf.at[pl.ds(0, CHIPS - 1)], g_send)
    wait_bytes(rbuf.at[pl.ds(0, CHIPS - 1)], r_send)
    for copy in to_slice + to_core + onward:
        copy.wait_send()
    for i in range(NZ // 2):

        @pl.when(par * (NZ // 2) + i != z)
        def _(i=i):
            wait_bytes(zsend.at[i], z_send.at[i])


def per_device(queries, image_cache, image_lists, cited_count, image_slot):
    vmem = pl.BlockSpec(memory_space=pltpu.VMEM)
    smem = pl.BlockSpec(memory_space=pltpu.SMEM)
    block = (CHIPS, BLOCK + GROUP, HD)
    result = pl.pallas_call(
        kernel,
        name="attend",
        out_shape=jax.ShapeDtypeStruct((GROUP, HD), jnp.float32),
        in_specs=[vmem, vmem, smem, smem, smem],
        out_specs=vmem,
        scratch_shapes=[
            pltpu.VMEM((CHIPS, BLOCK, HD), jnp.bfloat16),
            pltpu.VMEM((SEGS, KV_HERE, SEG, HD), jnp.bfloat16),
            pltpu.VMEM((SEGS, KV_HERE, SEG, HD), jnp.bfloat16),
            pltpu.VMEM((KV_HERE, TOK_SENT, HD), jnp.bfloat16),
            pltpu.VMEM((KV_HERE, TOK_SENT, HD), jnp.bfloat16),
            pltpu.VMEM((CHIPS, ROWS, SEGS * SEG), jnp.float32),
            pltpu.VMEM(block, jnp.float32),
            pltpu.VMEM(block, jnp.float32),
            pltpu.VMEM((NZ // 2, 2 * GROUP, HD), jnp.float32),
            pltpu.VMEM((NZ // 2, 2 * GROUP, HD), jnp.float32),
            pltpu.SemaphoreType.DMA,
            pltpu.SemaphoreType.DMA,
            pltpu.SemaphoreType.DMA((6,)),
            pltpu.SemaphoreType.DMA((6,)),
            pltpu.SemaphoreType.DMA,
            pltpu.SemaphoreType.DMA,
            pltpu.SemaphoreType.DMA((NZ // 2,)),
            pltpu.SemaphoreType.DMA((NZ // 2,)),
            pltpu.SemaphoreType.REGULAR,
        ],
        compiler_params=pltpu.CompilerParams(
            collective_id=0, has_side_effects=True, vmem_limit_bytes=32 * 2**20
        ),
    )(queries, image_cache, image_lists, cited_count, image_slot)
    return result.reshape(2, GROUP // 2 * HD)


def solution(mesh):
    return jax.shard_map(
        per_device,
        mesh=mesh,
        in_specs=(P("req", None), P("req", "tp", None), P(), P(), P()),
        out_specs=P("req", "tp"),
        check_vma=False,
    )
```

```python
import math

import jax
import jax.numpy as jnp
from jax import lax
from jax.experimental import pallas as pl
from jax.experimental.pallas import tpu as pltpu
from jax.sharding import PartitionSpec as P

KVH = 8
GROUP = 8
HD = 128
IMG_TOK = 1601
LISTS = 4
NX = 4
NY = 4
NZ = 16
CHIPS = NX * NY
REQS = 64
IMAGES = 32
TOK = 104
TOK_SENT = 112
SEG = 128
SEGS = 4
KV_HERE = KVH // 2
ROWS = 16
HALF = KV_HERE // 2 * ROWS
BLOCK = KV_HERE * ROWS
NEG = -1e30
SCALE = math.log2(math.e) / math.sqrt(HD)
MESH = pl.DeviceIdType.MESH


def wait_bytes(ref, sem):
    pltpu.make_async_copy(ref, ref, sem).wait()


def kernel(
    q_hbm, cache_hbm, lists_hbm, count_hbm, slot_hbm, out_ref,
    q_ref, cache_ref, lists_ref, count_ref, slot_ref,
    qbuf, kbuf, vbuf, ksend, vsend, bias, obuf, rbuf, zsend, zbuf,
    own_sem, g_send, g_recv, kv_send, kv_recv, r_send, r_recv, z_send, z_recv, z_near, z_far,
):
    req = lax.axis_index("req")
    z = lax.axis_index("tp")
    chip = lax.div(req, 2)
    core = lax.rem(req, 2)
    x = lax.div(chip, NY)
    y = lax.rem(chip, NY)
    par = lax.rem(z, 2)

    def device(x_, y_, c_, z_):
        return ((x_ * NY + y_) * 2 + c_, z_)

    def along_x(d):
        return lax.rem(x + d, NX)

    def along_y(d):
        return lax.rem(y + d, NY)

    def along_z(d):
        return lax.rem(z + d + NZ, NZ)

    other_core = device(x, y, 1 - core, z)
    partner = (along_z(1 - 2 * par), along_z(2 * par - 1))

    barrier = pltpu.get_barrier_semaphore()
    met = [other_core]
    met += [device(along_x(d), y, core, z) for d in (2, 1, 3)]
    met += [device(x, along_y(d), core, z) for d in (2, 1, 3)]
    met += [device(x, y, core, along_z(d)) for d in (-2, -1, 1, 2)]
    for there in met:
        pl.semaphore_signal(barrier, inc=1, device_id=there, device_id_type=MESH)

    own = [
        pltpu.make_async_copy(src, dst, own_sem.at[i])
        for i, (src, dst) in enumerate(
            (
                (q_hbm, q_ref),
                (cache_hbm, cache_ref),
                (lists_hbm, lists_ref),
                (count_hbm, count_ref),
                (slot_hbm, slot_ref),
            )
        )
    ]
    for copy in own:
        copy.start()

    own[0].wait()
    half = KV_HERE * GROUP * HD
    mine = q_ref[:, pl.ds(pl.multiple_of(par * half, half), half)].astype(jnp.float32)
    for k in range(KV_HERE):
        rows = [
            mine[r : r + 1, (k * GROUP + g) * HD : (k * GROUP + g + 1) * HD]
            for r in range(2)
            for g in range(GROUP)
        ]
        at = k % 2 * ROWS
        qbuf[x, y, k // 2, at : at + ROWS, :] = jnp.concatenate(rows, axis=0).astype(jnp.bfloat16)

    pl.semaphore_wait(barrier, len(met))
    for d in (-2, 2):
        there = device(x, y, core, along_z(d))
        pl.semaphore_signal(z_near, inc=1, device_id=there, device_id_type=MESH)

    def remote(src, dst, send, recv, there):
        return pltpu.make_async_remote_copy(
            src_ref=src, dst_ref=dst, send_sem=send, recv_sem=recv,
            device_id=there, device_id_type=MESH,
        )

    for d in (2, 1, 3):
        block = qbuf.at[x, y, 0]
        remote(block, block, g_send.at[0], g_recv.at[0], device(along_x(d), y, core, z)).start()
        block = qbuf.at[x, y, 1]
        remote(block, block, g_send.at[1], g_recv.at[1], device(x, along_y(d), core, z)).start()

    own[1].wait()
    tail = jnp.zeros((TOK_SENT - TOK, HD), jnp.bfloat16)
    sent = pl.ds(0, TOK_SENT)
    kv = ((ksend, kbuf, 0), (vsend, vbuf, KVH * HD))
    to_slice, to_core, onward = [], [], []
    for i, (outgoing, held, base) in enumerate(kv):
        for k in range(KV_HERE):
            at = pl.multiple_of(base + ((1 - par) * KV_HERE + k) * HD, HD)
            part = cache_ref[0, :, pl.ds(at, HD)]
            outgoing[k] = jnp.concatenate([part, tail], axis=0)
        for h in range(2):
            heads = pl.ds(2 * h, 2)
            to_slice.append(
                remote(
                    outgoing.at[heads], held.at[2, heads, sent], kv_send.at[4 * i + h],
                    kv_recv.at[4 * i + h], device(x, y, core, partner[h]),
                )
            )
            to_slice[-1].start()
        for k in range(KV_HERE):
            at = pl.multiple_of(base + (par * KV_HERE + k) * HD, HD)
            part = cache_ref[0, :, pl.ds(at, HD)]
            held[0, k, :TOK_SENT, :] = jnp.concatenate([part, tail], axis=0)
        to_core.append(
            remote(
                held.at[0, :, sent], held.at[1, :, sent], kv_send.at[4 * i + 2],
                kv_recv.at[4 * i + 2], other_core,
            )
        )
        to_core[-1].start()
        onward.append(
            remote(
                held.at[2, :, sent], held.at[3, :, sent], kv_send.at[4 * i + 3],
                kv_recv.at[4 * i + 3], other_core,
            )
        )

    wait_bytes(qbuf.at[pl.ds(0, NX - 1), 0, 0], g_recv.at[0])
    for d in (2, 1, 3):
        block = qbuf.at[:, y, 0]
        remote(block, block, g_send.at[2], g_recv.at[2], device(x, along_y(d), core, z)).start()
    wait_bytes(qbuf.at[0, pl.ds(0, NY - 1), 1], g_recv.at[1])
    for d in (2, 1, 3):
        block = qbuf.at[x, :, 1]
        remote(block, block, g_send.at[3], g_recv.at[3], device(along_x(d), y, core, z)).start()

    pl.semaphore_wait(z_near, 2)
    for d in (-4, 4):
        there = device(x, y, core, along_z(d))
        pl.semaphore_signal(z_far, inc=1, device_id=there, device_id_type=MESH)

    to_slice[0].wait_recv()
    to_slice[1].wait_recv()
    onward[0].start()

    pad = jnp.zeros((SEG - TOK_SENT, HD), jnp.bfloat16)
    for s in range(SEGS):
        for k in range(KV_HERE):
            kbuf[s, k, TOK_SENT:, :] = pad
            vbuf[s, k, TOK_SENT:, :] = pad

    for copy in own[2:]:
        copy.wait()
    lanes = lax.broadcasted_iota(jnp.int32, (GROUP, SEG), 1)
    seen = []
    for slice_ in (z, *partner):
        ok = (lanes < TOK) & (slice_ * TOK + lanes < IMG_TOK)
        seen.append(jnp.where(ok, 0.0, NEG))

    @pl.loop(0, CHIPS)
    def _(d):
        for r in range(2):
            request = 4 * d + 2 * core + r
            cited = count_ref[request]
            hit = [jnp.int32(0), jnp.int32(0)]
            for j in range(LISTS):
                slot = slot_ref[lists_ref[j, request]]
                here = jnp.where(j < cited, 1, 0)
                for i, stored in enumerate((req, 2 * chip + 1 - core)):
                    hit[i] = hit[i] + jnp.where(slot == stored, here, 0)
            for i in range(2):
                level = jnp.where(hit[i] > 0, 0.0, NEG)
                for s in range(3):
                    at = (2 * s + i) * SEG
                    bias[lax.div(d, NY), lax.rem(d, NY), r * GROUP : (r + 1) * GROUP, at : at + SEG] = seen[s] + level

    to_slice[2].wait_recv()
    to_slice[3].wait_recv()
    onward[1].start()
    wait_bytes(qbuf.at[:, pl.ds(0, NY - 1), 0], g_recv.at[2])
    wait_bytes(qbuf.at[pl.ds(0, NX - 1), :, 1], g_recv.at[3])
    to_core[0].wait_recv()
    onward[0].wait_recv()

    some = 2 * NY
    lane = lax.broadcasted_iota(jnp.int32, (some, GROUP, HD), 2)
    for part in range(2):
        columns = (along_x(2), along_x(1)) if part == 0 else (along_x(3), x)
        levels = jnp.concatenate([bias[c].reshape(NY * ROWS, 6 * SEG) for c in columns], axis=0)
        softmax = []
        for k in range(KV_HERE):
            at = slice(k % 2 * ROWS, (k % 2 + 1) * ROWS)
            queries = jnp.concatenate(
                [qbuf[c, :, k // 2, at, :].reshape(NY * ROWS, HD) for c in columns], axis=0
            )
            keys = kbuf[:, k].reshape(SEGS * SEG, HD)
            scores = lax.dot_general(
                queries, keys, (((1,), (1,)), ((), ())), preferred_element_type=jnp.float32
            )
            near = levels[:, : 2 * SEG]
            far = levels[:, (2 + 2 * (k // 2)) * SEG : (4 + 2 * (k // 2)) * SEG]
            scores = scores * SCALE + jnp.concatenate([near, far], axis=1)
            peak = jnp.max(scores, axis=1, keepdims=True)
            weights = jnp.exp2(scores - peak)
            total = jnp.sum(weights, axis=1, keepdims=True)
            high = weights.astype(jnp.bfloat16)
            low = (weights - high.astype(jnp.float32)).astype(jnp.bfloat16)
            softmax.append((high, low, peak, total))
        if part == 0:
            to_core[1].wait_recv()
            onward[1].wait_recv()
        stat = jnp.zeros((some, GROUP, HD), jnp.float32)
        for k in range(KV_HERE):
            high, low, peak, total = softmax[k]
            values = vbuf[:, k].reshape(SEGS * SEG, HD)
            weighted = jnp.dot(high, values, preferred_element_type=jnp.float32)
            weighted += jnp.dot(low, values, preferred_element_type=jnp.float32)
            weighted = (weighted / total).reshape(2, NY, ROWS, HD)
            for i, c in enumerate(columns):
                obuf[pl.ds(c * NY, NY), k * ROWS : (k + 1) * ROWS, :] = weighted[i]
            size = (peak + jnp.log2(total)).reshape(some, 2, GROUP, 1)
            for r in range(2):
                stat = jnp.where(lane == r * KV_HERE + k, size[:, r], stat)
        for i, c in enumerate(columns):
            obuf[pl.ds(c * NY, NY), BLOCK:, :] = stat[i * NY : (i + 1) * NY]
        for i, c in enumerate(columns):
            for d in (2, 1, 3, 0):
                if part == 1 and i == 1 and d == 0:
                    continue
                row = along_y(d)
                remote(obuf.at[c * NY + row], rbuf.at[chip], r_send, r_recv, device(c, row, core, z)).start()
    rbuf[chip] = obuf[chip]
    pl.semaphore_wait(z_far, 2)
    wait_bytes(rbuf.at[pl.ds(0, CHIPS - 1)], r_recv)

    sizes = rbuf[:, BLOCK:, :]
    largest = jnp.max(sizes, axis=0)
    share = jnp.exp2(sizes - largest[None])
    total = jnp.sum(share, axis=0)
    share = share / total[None]
    size = largest + jnp.log2(total)
    low_rows = lax.broadcasted_iota(jnp.int32, (GROUP, HD), 0) < GROUP // 2
    for k in range(KV_HERE):
        both, logs = [], []
        for r in range(2):
            at = k * ROWS + r * GROUP
            col = r * KV_HERE + k
            result = jnp.zeros((GROUP, HD), jnp.float32)
            for s in range(CHIPS):
                result += rbuf[s, at : at + GROUP, :] * share[s, :, col : col + 1]
            both.append(result)
            logs.append(jnp.broadcast_to(size[:, col : col + 1], (GROUP, HD)))
        for h in range(2):
            for row, (a, b) in ((0, both), (GROUP, logs)):
                if h == 0:
                    tile = jnp.where(low_rows, a, pltpu.roll(b, GROUP // 2, 0))
                else:
                    tile = jnp.where(low_rows, pltpu.roll(a, GROUP // 2, 0), b)
                zsend[2 * k + h, row : row + GROUP, :] = tile
            there = 2 * (par * KV_HERE + k) + h

            @pl.when(there != z)
            def _(k=k, h=h, there=there):
                remote(
                    zsend.at[2 * k + h], zbuf.at[lax.div(z, 2)], z_send.at[2 * k + h],
                    z_recv.at[lax.div(z, 2)], device(x, y, core, there),
                ).start()

            @pl.when(there == z)
            def _(k=k, h=h):
                zbuf[lax.div(z, 2)] = zsend[2 * k + h]

    theirs = lax.div(z, NZ // 2)
    for i in range(NZ // 2):

        @pl.when(2 * i + theirs != z)
        def _(i=i):
            wait_bytes(zbuf.at[i], z_recv.at[i])

    sizes = zbuf[:, GROUP:, :]
    largest = jnp.max(sizes, axis=0)
    share = jnp.exp2(sizes - largest[None])
    out_ref[...] = jnp.sum(zbuf[:, :GROUP, :] * share, axis=0) / jnp.sum(share, axis=0)

    wait_bytes(qbuf.at[pl.ds(0, NX - 1), 0, 0], g_send.at[0])
    wait_bytes(qbuf.at[0, pl.ds(0, NY - 1), 1], g_send.at[1])
    wait_bytes(qbuf.at[:, pl.ds(0, NY - 1), 0], g_send.at[2])
    wait_bytes(qbuf.at[pl.ds(0, NX - 1), :, 1], g_send.at[3])
    wait_bytes(rbuf.at[pl.ds(0, CHIPS - 1)], r_send)
    for copy in to_slice + to_core + onward:
        copy.wait_send()
    for i in range(NZ // 2):

        @pl.when(par * (NZ // 2) + i != z)
        def _(i=i):
            wait_bytes(zsend.at[i], z_send.at[i])


def per_device(queries, image_cache, image_lists, cited_count, image_slot):
    here = pl.BlockSpec(memory_space=pl.ANY)
    block = (CHIPS, BLOCK + GROUP, HD)
    held = (SEGS, KV_HERE, SEG, HD)
    result = pl.pallas_call(
        kernel,
        name="attend",
        out_shape=jax.ShapeDtypeStruct((GROUP, HD), jnp.float32),
        in_specs=[here] * 5,
        out_specs=pl.BlockSpec(memory_space=pltpu.VMEM),
        scratch_shapes=[
            pltpu.VMEM(queries.shape, jnp.bfloat16),
            pltpu.VMEM(image_cache.shape, jnp.bfloat16),
            pltpu.SMEM((LISTS, REQS), jnp.int32),
            pltpu.SMEM((REQS,), jnp.int32),
            pltpu.SMEM((IMAGES,), jnp.int32),
            pltpu.VMEM((NX, NY, 2, HALF, HD), jnp.bfloat16),
            pltpu.VMEM(held, jnp.bfloat16),
            pltpu.VMEM(held, jnp.bfloat16),
            pltpu.VMEM((KV_HERE, TOK_SENT, HD), jnp.bfloat16),
            pltpu.VMEM((KV_HERE, TOK_SENT, HD), jnp.bfloat16),
            pltpu.VMEM((NX, NY, ROWS, 6 * SEG), jnp.float32),
            pltpu.VMEM(block, jnp.float32),
            pltpu.VMEM(block, jnp.float32),
            pltpu.VMEM((NZ // 2, 2 * GROUP, HD), jnp.float32),
            pltpu.VMEM((NZ // 2, 2 * GROUP, HD), jnp.float32),
            pltpu.SemaphoreType.DMA((5,)),
            pltpu.SemaphoreType.DMA((4,)),
            pltpu.SemaphoreType.DMA((4,)),
            pltpu.SemaphoreType.DMA((8,)),
            pltpu.SemaphoreType.DMA((8,)),
            pltpu.SemaphoreType.DMA,
            pltpu.SemaphoreType.DMA,
            pltpu.SemaphoreType.DMA((NZ // 2,)),
            pltpu.SemaphoreType.DMA((NZ // 2,)),
            pltpu.SemaphoreType.REGULAR,
            pltpu.SemaphoreType.REGULAR,
        ],
        compiler_params=pltpu.CompilerParams(
            collective_id=0, has_side_effects=True, vmem_limit_bytes=60 * 2**20
        ),
    )(queries, image_cache, image_lists.T, cited_count, image_slot)
    return result.reshape(2, GROUP // 2 * HD)


def solution(mesh):
    return jax.shard_map(
        per_device,
        mesh=mesh,
        in_specs=(P("req", None), P("req", "tp", None), P(), P(), P()),
        out_specs=P("req", "tp"),
        check_vma=False,
    )
```

```python
import math

import jax
import jax.numpy as jnp
from jax import lax
from jax.experimental import pallas as pl
from jax.experimental.pallas import tpu as pltpu
from jax.sharding import PartitionSpec as P

KVH = 8
GROUP = 8
HD = 128
IMG_TOK = 1601
LISTS = 4
NX = 4
NY = 4
NZ = 16
CHIPS = NX * NY
REQS = 64
IMAGES = 32
TOK = 104
TOK_SENT = 112
SEG = 128
SEGS = 4
KV_HERE = KVH // 2
ROWS = 16
NEG = -1e30
SCALE = math.log2(math.e) / math.sqrt(HD)
MESH = pl.DeviceIdType.MESH


def wait_bytes(ref, sem):
    pltpu.make_async_copy(ref, ref, sem).wait()


def kernel(
    q_hbm, cache_hbm, lists_hbm, count_hbm, slot_hbm, out_ref,
    q_ref, cache_ref, lists_ref, count_ref, slot_ref,
    qbuf, kvbuf, kvsend, bias, first_out, first_in, rest_out, rest_in, zsend, zbuf,
    own_sem, q_send, q_recv, kv_send, kv_recv, r_send, r_recv, z_send, z_recv, z_near, z_far,
):
    req = lax.axis_index("req")
    z = lax.axis_index("tp")
    chip = lax.div(req, 2)
    core = lax.rem(req, 2)
    x = lax.div(chip, NY)
    y = lax.rem(chip, NY)
    par = lax.rem(z, 2)

    def device(x_, y_, c_, z_):
        return ((x_ * NY + y_) * 2 + c_, z_)

    def along_x(d):
        return lax.rem(x + d, NX)

    def along_y(d):
        return lax.rem(y + d, NY)

    def along_z(d):
        return lax.rem(z + d + NZ, NZ)

    other_core = device(x, y, 1 - core, z)
    partner = (along_z(1 - 2 * par), along_z(2 * par - 1))

    def key_head(k, par_):
        return 2 * k + 1 - par_

    barrier = pltpu.get_barrier_semaphore()
    met = [device(along_x(d), y, core, z) for d in (2, 1, 3)]
    met += [device(x, along_y(d), core, z) for d in (2, 1, 3)]
    met += [device(x, y, core, along_z(d)) for d in (-2, -1, 1, 2)]
    met += [other_core]
    for there in met:
        pl.semaphore_signal(barrier, inc=1, device_id=there, device_id_type=MESH)

    own = [
        pltpu.make_async_copy(src, dst, own_sem.at[i])
        for i, (src, dst) in enumerate(
            (
                (q_hbm, q_ref),
                (cache_hbm, cache_ref),
                (lists_hbm, lists_ref),
                (count_hbm, count_ref),
                (slot_hbm, slot_ref),
            )
        )
    ]
    for copy in own:
        copy.start()

    own[0].wait()
    for k in range(KV_HERE):
        width = GROUP * HD
        at = pl.multiple_of(key_head(k, par) * width, width)
        mine = q_ref[:, pl.ds(at, width)].astype(jnp.float32)
        rows = [mine[r : r + 1, g * HD : (g + 1) * HD] for r in range(2) for g in range(GROUP)]
        qbuf[x, y, k] = jnp.concatenate(rows, axis=0).astype(jnp.bfloat16)

    pl.semaphore_wait(barrier, len(met))

    def remote(src, dst, send, recv, there):
        return pltpu.make_async_remote_copy(
            src_ref=src, dst_ref=dst, send_sem=send, recv_sem=recv,
            device_id=there, device_id_type=MESH,
        )

    rest = pl.ds(1, KV_HERE - 1)
    for d in (2, 1, 3):
        block = qbuf.at[x, y, 0]
        remote(block, block, q_send.at[0], q_recv.at[0], device(along_x(d), y, core, z)).start()
    for d in (2, 1, 3):
        block = qbuf.at[x, y, rest]
        remote(block, block, q_send.at[1], q_recv.at[1], device(x, along_y(d), core, z)).start()

    for d in (-2, 2):
        there = device(x, y, core, along_z(d))
        pl.semaphore_signal(z_near, inc=1, device_id=there, device_id_type=MESH)

    own[1].wait()
    tail = jnp.zeros((TOK_SENT - TOK, HD), jnp.bfloat16)
    sent = pl.ds(0, TOK_SENT)

    def stored(k, par_, i):
        at = pl.multiple_of((i * KVH + key_head(k, par_)) * HD, HD)
        return jnp.concatenate([cache_ref[0, :, pl.ds(at, HD)], tail], axis=0)

    def kv_copy(i, src, dst, there):
        return remote(src, dst, kv_send.at[i], kv_recv.at[i], there)

    neighbour = [device(x, y, core, partner[h]) for h in range(2)]
    late = pl.ds(2, 2)
    to_slice = [
        kv_copy(0, kvsend.at[0, 0], kvbuf.at[2, 0, 0, sent], neighbour[0]),
        kv_copy(1, kvsend.at[0, 1], kvbuf.at[2, 0, 1, sent], neighbour[0]),
        kv_copy(2, kvsend.at[1], kvbuf.at[2, 1, :, sent], neighbour[0]),
        kv_copy(3, kvsend.at[late], kvbuf.at[2, late, :, sent], neighbour[1]),
    ]
    to_core = [
        kv_copy(4, kvbuf.at[0, 0, 0, sent], kvbuf.at[1, 0, 0, sent], other_core),
        kv_copy(5, kvbuf.at[0, 0, 1, sent], kvbuf.at[1, 0, 1, sent], other_core),
        kv_copy(6, kvbuf.at[0, rest, :, sent], kvbuf.at[1, rest, :, sent], other_core),
    ]
    onward = [
        kv_copy(7, kvbuf.at[2, 0, 0, sent], kvbuf.at[3, 0, 0, sent], other_core),
        kv_copy(8, kvbuf.at[2, 0, 1, sent], kvbuf.at[3, 0, 1, sent], other_core),
        kv_copy(9, kvbuf.at[2, 1, :, sent], kvbuf.at[3, 1, :, sent], other_core),
        kv_copy(10, kvbuf.at[2, late, :, sent], kvbuf.at[3, late, :, sent], other_core),
    ]
    for i in range(2):
        kvsend[0, i] = stored(0, 1 - par, i)
        to_slice[i].start()
    for i in range(2):
        kvbuf[0, 0, i, :TOK_SENT, :] = stored(0, par, i)
        to_core[i].start()
    for k in range(1, KV_HERE):
        for i in range(2):
            kvsend[k, i] = stored(k, 1 - par, i)
    to_slice[2].start()
    to_slice[3].start()
    for k in range(1, KV_HERE):
        for i in range(2):
            kvbuf[0, k, i, :TOK_SENT, :] = stored(k, par, i)
    to_core[2].start()

    pad = jnp.zeros((SEG - TOK_SENT, HD), jnp.bfloat16)
    for s in range(SEGS):
        for k in range(KV_HERE):
            for i in range(2):
                kvbuf[s, k, i, TOK_SENT:, :] = pad

    for copy in own[2:]:
        copy.wait()
    lanes = lax.broadcasted_iota(jnp.int32, (GROUP, SEG), 1)
    seen = []
    for slice_ in (z, *partner):
        ok = (lanes < TOK) & (slice_ * TOK + lanes < IMG_TOK)
        seen.append(jnp.where(ok, 0.0, NEG))

    @pl.loop(0, CHIPS)
    def _(d):
        for r in range(2):
            request = 4 * d + 2 * core + r
            cited = count_ref[request]
            hit = [jnp.int32(0), jnp.int32(0)]
            for j in range(LISTS):
                slot = slot_ref[lists_ref[j, request]]
                here = jnp.where(j < cited, 1, 0)
                for i, stored_here in enumerate((req, 2 * chip + 1 - core)):
                    hit[i] = hit[i] + jnp.where(slot == stored_here, here, 0)
            for i in range(2):
                level = jnp.where(hit[i] > 0, 0.0, NEG)
                for s in range(3):
                    at = (2 * s + i) * SEG
                    bias[d, r * GROUP : (r + 1) * GROUP, at : at + SEG] = seen[s] + level

    wait_bytes(qbuf.at[pl.ds(0, NX - 1), 0, 0], q_recv.at[0])
    for d in (2, 1, 3):
        block = qbuf.at[:, y, 0]
        remote(block, block, q_send.at[2], q_recv.at[2], device(x, along_y(d), core, z)).start()
    wait_bytes(qbuf.at[0, pl.ds(0, NY - 1), rest], q_recv.at[1])
    for d in (2, 1, 3):
        block = qbuf.at[x, :, rest]
        remote(block, block, q_send.at[3], q_recv.at[3], device(along_x(d), y, core, z)).start()

    for i in range(2):
        to_slice[i].wait_recv()
        onward[i].start()

    pl.semaphore_wait(z_near, 2)
    for d in (-4, 4):
        there = device(x, y, core, along_z(d))
        pl.semaphore_signal(z_far, inc=1, device_id=there, device_id_type=MESH)

    def scored(k, columns):
        queries = jnp.concatenate([qbuf[c, :, k].reshape(NY * ROWS, HD) for c in columns], axis=0)
        keys = kvbuf[:, k, 0].reshape(SEGS * SEG, HD)
        scores = lax.dot_general(
            queries, keys, (((1,), (1,)), ((), ())), preferred_element_type=jnp.float32
        )
        far = (2 + 2 * (k // 2)) * SEG
        allowed = [
            jnp.concatenate(
                [bias[pl.ds(c * NY, NY), :, : 2 * SEG], bias[pl.ds(c * NY, NY), :, far : far + 2 * SEG]],
                axis=2,
            ).reshape(NY * ROWS, SEGS * SEG)
            for c in columns
        ]
        scores = scores * SCALE + jnp.concatenate(allowed, axis=0)
        peak = jnp.max(scores, axis=1, keepdims=True)
        weights = jnp.exp2(scores - peak)
        total = jnp.sum(weights, axis=1, keepdims=True)
        high = weights.astype(jnp.bfloat16)
        low = (weights - high.astype(jnp.float32)).astype(jnp.bfloat16)
        return high, low, peak, total

    def weigh(ks, columns, softmax, out):
        some = len(columns) * NY
        lane = lax.broadcasted_iota(jnp.int32, (some, GROUP, HD), 2)
        stat = jnp.zeros((some, GROUP, HD), jnp.float32)
        for n, k in enumerate(ks):
            high, low, peak, total = softmax[n]
            values = kvbuf[:, k, 1].reshape(SEGS * SEG, HD)
            weighted = jnp.dot(high, values, preferred_element_type=jnp.float32)
            weighted += jnp.dot(low, values, preferred_element_type=jnp.float32)
            weighted = (weighted / total).reshape(some, ROWS, HD)
            for i, c in enumerate(columns):
                out[pl.ds(c * NY, NY), n * ROWS : (n + 1) * ROWS, :] = weighted[i * NY : (i + 1) * NY]
            size = (peak + jnp.log2(total)).reshape(some, 2, GROUP, 1)
            for r in range(2):
                stat = jnp.where(lane == r * len(ks) + n, size[:, r], stat)
        for i, c in enumerate(columns):
            out[pl.ds(c * NY, NY), len(ks) * ROWS :, :] = stat[i * NY : (i + 1) * NY]

    def go_home(columns, out, arrived, i):
        for c, skip in columns:
            for d in (2, 1, 3) if skip else (2, 1, 3, 0):
                row = along_y(d)
                there = device(c, row, core, z)
                remote(out.at[c * NY + row], arrived.at[chip], r_send.at[i], r_recv.at[i], there).start()

    far_columns, near_columns = [along_x(2), along_x(1)], [along_x(3), x]
    wait_bytes(qbuf.at[:, pl.ds(0, NY - 1), 0], q_recv.at[2])
    to_core[0].wait_recv()
    onward[0].wait_recv()
    softmax = [scored(0, columns) for columns in (far_columns, near_columns)]
    to_core[1].wait_recv()
    onward[1].wait_recv()
    weigh([0], far_columns, softmax[:1], first_out)
    go_home([(c, False) for c in far_columns], first_out, first_in, 0)
    weigh([0], near_columns, softmax[1:], first_out)
    go_home([(near_columns[0], False), (x, True)], first_out, first_in, 0)
    first_in[chip] = first_out[chip]

    for i in range(2, 4):
        to_slice[i].wait_recv()
        onward[i].start()
    wait_bytes(qbuf.at[pl.ds(0, NX - 1), :, rest], q_recv.at[3])
    to_core[2].wait_recv()
    onward[2].wait_recv()
    onward[3].wait_recv()
    later = list(range(1, KV_HERE))
    for columns in (far_columns, near_columns):
        weigh(later, columns, [scored(k, columns) for k in later], rest_out)
        go_home([(columns[0], False), (columns[1], columns is near_columns)], rest_out, rest_in, 1)
    rest_in[chip] = rest_out[chip]

    low_rows = lax.broadcasted_iota(jnp.int32, (GROUP, HD), 0) < GROUP // 2

    def spread(ks, arrived):
        data = len(ks) * ROWS
        sizes = arrived[:, data:, :]
        largest = jnp.max(sizes, axis=0)
        share = jnp.exp2(sizes - largest[None])
        total = jnp.sum(share, axis=0)
        share = share / total[None]
        size = largest + jnp.log2(total)
        for n, k in enumerate(ks):
            both, logs = [], []
            for r in range(2):
                at = n * ROWS + r * GROUP
                col = r * len(ks) + n
                parts = [arrived[s, at : at + GROUP, :] * share[s, :, col : col + 1] for s in range(CHIPS)]
                while len(parts) > 1:
                    parts = [a + b for a, b in zip(parts[::2], parts[1::2])]
                both.append(parts[0])
                logs.append(jnp.broadcast_to(size[:, col : col + 1], (GROUP, HD)))
            for h in range(2):
                for row, (a, b) in ((0, both), (GROUP, logs)):
                    if h == 0:
                        tile = jnp.where(low_rows, a, pltpu.roll(b, GROUP // 2, 0))
                    else:
                        tile = jnp.where(low_rows, pltpu.roll(a, GROUP // 2, 0), b)
                    zsend[2 * k + h, row : row + GROUP, :] = tile
                there = 2 * key_head(k, par) + h

                @pl.when(there != z)
                def _():
                    remote(
                        zsend.at[2 * k + h], zbuf.at[lax.div(z, 2)], z_send.at[2 * k + h],
                        z_recv.at[lax.div(z, 2)], device(x, y, core, there),
                    ).start()

                @pl.when(there == z)
                def _():
                    zbuf[lax.div(z, 2)] = zsend[2 * k + h]

    pl.semaphore_wait(z_far, 2)
    wait_bytes(first_in.at[pl.ds(0, CHIPS - 1)], r_recv.at[0])
    spread([0], first_in)
    wait_bytes(rest_in.at[pl.ds(0, CHIPS - 1)], r_recv.at[1])
    spread(later, rest_in)

    theirs = 1 - lax.rem(lax.div(z, 2), 2)
    for i in range(NZ // 2):

        @pl.when(2 * i + theirs != z)
        def _(i=i):
            wait_bytes(zbuf.at[i], z_recv.at[i])

    sizes = zbuf[:, GROUP:, :]
    largest = jnp.max(sizes, axis=0)
    share = jnp.exp2(sizes - largest[None])
    out_ref[...] = jnp.sum(zbuf[:, :GROUP, :] * share, axis=0) / jnp.sum(share, axis=0)

    wait_bytes(qbuf.at[pl.ds(0, NX - 1), 0, 0], q_send.at[0])
    wait_bytes(qbuf.at[0, pl.ds(0, NY - 1), rest], q_send.at[1])
    wait_bytes(qbuf.at[:, pl.ds(0, NY - 1), 0], q_send.at[2])
    wait_bytes(qbuf.at[pl.ds(0, NX - 1), :, rest], q_send.at[3])
    wait_bytes(first_in.at[pl.ds(0, CHIPS - 1)], r_send.at[0])
    wait_bytes(rest_in.at[pl.ds(0, CHIPS - 1)], r_send.at[1])
    for copy in to_slice + to_core + onward:
        copy.wait_send()
    for k in range(KV_HERE):
        for h in range(2):

            @pl.when(2 * key_head(k, par) + h != z)
            def _():
                wait_bytes(zsend.at[2 * k + h], z_send.at[2 * k + h])


def per_device(queries, image_cache, image_lists, cited_count, image_slot):
    here = pl.BlockSpec(memory_space=pl.ANY)
    first = (CHIPS, ROWS + GROUP, HD)
    rest = (CHIPS, (KV_HERE - 1) * ROWS + GROUP, HD)
    result = pl.pallas_call(
        kernel,
        name="attend",
        out_shape=jax.ShapeDtypeStruct((GROUP, HD), jnp.float32),
        in_specs=[here] * 5,
        out_specs=pl.BlockSpec(memory_space=pltpu.VMEM),
        scratch_shapes=[
            pltpu.VMEM(queries.shape, jnp.bfloat16),
            pltpu.VMEM(image_cache.shape, jnp.bfloat16),
            pltpu.SMEM((LISTS, REQS), jnp.int32),
            pltpu.SMEM((REQS,), jnp.int32),
            pltpu.SMEM((IMAGES,), jnp.int32),
            pltpu.VMEM((NX, NY, KV_HERE, ROWS, HD), jnp.bfloat16),
            pltpu.VMEM((SEGS, KV_HERE, 2, SEG, HD), jnp.bfloat16),
            pltpu.VMEM((KV_HERE, 2, TOK_SENT, HD), jnp.bfloat16),
            pltpu.VMEM((CHIPS, ROWS, 6 * SEG), jnp.float32),
            pltpu.VMEM(first, jnp.float32),
            pltpu.VMEM(first, jnp.float32),
            pltpu.VMEM(rest, jnp.float32),
            pltpu.VMEM(rest, jnp.float32),
            pltpu.VMEM((NZ // 2, 2 * GROUP, HD), jnp.float32),
            pltpu.VMEM((NZ // 2, 2 * GROUP, HD), jnp.float32),
            pltpu.SemaphoreType.DMA((5,)),
            pltpu.SemaphoreType.DMA((4,)),
            pltpu.SemaphoreType.DMA((4,)),
            pltpu.SemaphoreType.DMA((11,)),
            pltpu.SemaphoreType.DMA((11,)),
            pltpu.SemaphoreType.DMA((2,)),
            pltpu.SemaphoreType.DMA((2,)),
            pltpu.SemaphoreType.DMA((NZ // 2,)),
            pltpu.SemaphoreType.DMA((NZ // 2,)),
            pltpu.SemaphoreType.REGULAR,
            pltpu.SemaphoreType.REGULAR,
        ],
        compiler_params=pltpu.CompilerParams(
            collective_id=0, has_side_effects=True, vmem_limit_bytes=60 * 2**20
        ),
    )(queries, image_cache, image_lists.T, cited_count, image_slot)
    return result.reshape(2, GROUP // 2 * HD)


def solution(mesh):
    return jax.shard_map(
        per_device,
        mesh=mesh,
        in_specs=(P("req", None), P("req", "tp", None), P(), P(), P()),
        out_specs=P("req", "tp"),
        check_vma=False,
    )
```

```python
import math

import jax
import jax.numpy as jnp
from jax import lax
from jax.experimental import pallas as pl
from jax.experimental.pallas import tpu as pltpu
from jax.sharding import PartitionSpec as P

KVH = 8
GROUP = 8
HD = 128
IMG_TOK = 1601
LISTS = 4
SIDE = 4
NZ = 16
REQS = 64
IMAGES = 32
TOK = 104
TOK_SENT = 112
SEG = 128
LINE = 2 * SIDE
ROWS = 16
STAGES = KVH // 2
PAIRS = (0, 1, 3, 2)
NEG = -1e30
SCALE = math.log2(math.e) / math.sqrt(HD)
MESH = pl.DeviceIdType.MESH
FIRST_LATE = NZ // 2
GREETED = tuple(min(n, 8) if n < 12 else 7 if n == 12 else 6 for n in range(NZ))


def wait_bytes(ref, sem):
    pltpu.make_async_copy(ref, ref, sem).wait()


def kernel(
    q_hbm, cache_hbm, lists_hbm, count_hbm, slot_hbm, out_ref,
    q_ref, cache_ref, lists_ref, count_ref, slot_ref,
    q_own, kv_own, q_buf, kv_buf, bias, home_out, home_in, z_out, z_in,
    own_sem, q_send, q_recv, kv_send, kv_recv, h_send, h_recv, z_send, z_recv, z_met,
):
    req = lax.axis_index("req")
    z = lax.axis_index("tp")
    core = lax.rem(req, 2)
    x = lax.div(req, 2 * SIDE)
    y = lax.rem(lax.div(req, 2), SIDE)
    even = core == 0

    def device(x_, y_, c_, z_=z):
        return ((x_ * SIDE + y_) * 2 + c_, z_)

    def along_x(d, c_):
        return device(lax.rem(x + d, SIDE), y, c_)

    def along_y(d, c_):
        return device(x, lax.rem(y + d, SIDE), c_)

    def along_z(d):
        return device(x, y, core, lax.rem(z + d + NZ, NZ))

    other_core = device(x, y, 1 - core)
    kv_place = jnp.where(even, x, y)
    q_place = jnp.where(even, y, x)

    barrier = pltpu.get_barrier_semaphore()
    met = [line(d, c_) for d in (2, 1, 3) for line in (along_x, along_y) for c_ in range(2)]
    met += [other_core]
    for there in met:
        pl.semaphore_signal(barrier, inc=1, device_id=there, device_id_type=MESH)
    late = z >= FIRST_LATE

    def near(d):
        return late & (z + d >= FIRST_LATE) & (z + d < NZ)

    for d in (-2, -1, 1, 2):

        @pl.when(near(d))
        def _():
            pl.semaphore_signal(barrier, inc=1, device_id=along_z(d), device_id_type=MESH)

    for n in range(NZ - 1, 0, -1):

        @pl.when(z < GREETED[n])
        def _():
            there = device(x, y, core, n)
            pl.semaphore_signal(barrier, inc=1, device_id=there, device_id_type=MESH)

    own = [
        pltpu.make_async_copy(src, dst, own_sem.at[i])
        for i, (src, dst) in enumerate(
            (
                (q_hbm, q_ref),
                (cache_hbm, cache_ref),
                (lists_hbm, lists_ref),
                (count_hbm, count_ref),
                (slot_hbm, slot_ref),
            )
        )
    ]
    for copy in own:
        copy.start()

    own[0].wait()
    for s in range(STAGES):
        for c in range(2):
            first = (2 * PAIRS[s] + c) * GROUP * HD
            mine = q_ref[:, first : first + GROUP * HD].astype(jnp.float32)
            rows = [mine[r : r + 1, g * HD : (g + 1) * HD] for r in range(2) for g in range(GROUP)]
            q_own[c, s] = jnp.concatenate(rows, axis=0).astype(jnp.bfloat16)
    q_buf[2 * q_place + core] = q_own[core]

    own[1].wait()
    tail = jnp.zeros((TOK_SENT - TOK, HD), jnp.bfloat16)
    for k in range(KVH):
        for i in range(2):
            first = (i * KVH + k) * HD
            kv_own[k, i] = jnp.concatenate([cache_ref[0, :, first : first + HD], tail], axis=0)
    pad = jnp.zeros((SEG - TOK_SENT, HD), jnp.bfloat16)
    for s in range(STAGES):
        kv_buf[s, 2 * kv_place + core, :, :TOK_SENT, :] = kv_own[2 * PAIRS[s] + core]
        for n in range(LINE):
            for i in range(2):
                kv_buf[s, n, i, TOK_SENT:, :] = pad

    greeted = jnp.int32(len(met))
    for d in (-2, -1, 1, 2):
        greeted = greeted + jnp.where(near(d), 1, 0)
    for n in range(1, NZ):
        greeted = greeted + jnp.where(z == n, GREETED[n], 0)
    pl.semaphore_wait(barrier, greeted)

    def send(src, dst, sems, n, there):
        send_sem, recv_sem = sems
        pltpu.make_async_remote_copy(
            src_ref=src, dst_ref=dst, send_sem=send_sem.at[n], recv_sem=recv_sem.at[n],
            device_id=there, device_id_type=MESH,
        ).start()

    sent = pl.ds(0, TOK_SENT)

    def send_kv(n, s, part):
        for d in (2, 1, 3):
            for c, line, place in ((0, along_x, x), (1, along_y, y)):
                src, dst = kv_own.at[2 * PAIRS[s] + c, part], kv_buf.at[s, 2 * place + core, part, sent]
                send(src, dst, (kv_send, kv_recv), n, line(d, c))
        place = jnp.where(even, y, x)
        src, dst = kv_own.at[2 * PAIRS[s] + 1 - core, part], kv_buf.at[s, 2 * place + core, part, sent]
        send(src, dst, (kv_send, kv_recv), n, other_core)

    def send_q(n, stages):
        for d in (2, 1, 3):
            for c, line, place in ((0, along_y, y), (1, along_x, x)):
                src, dst = q_own.at[c, stages], q_buf.at[2 * place + core, stages]
                send(src, dst, (q_send, q_recv), n, line(d, c))
        place = jnp.where(even, x, y)
        src, dst = q_own.at[1 - core, stages], q_buf.at[2 * place + core, stages]
        send(src, dst, (q_send, q_recv), n, other_core)

    both = slice(None)
    later = pl.ds(1, STAGES - 1)
    send_kv(0, 0, 0)
    send_q(0, 0)
    send_kv(1, 0, 1)
    send_q(1, later)
    send_kv(2, 1, both)

    def tell(n, there):
        pl.semaphore_signal(z_met.at[n], inc=1, device_id=device(x, y, core, there), device_id_type=MESH)

    def pass_on(n, step):
        for d in (-step, step):

            @pl.when(near(d))
            def _():
                tell(n, z + d)

    def told(n, step):
        count = jnp.where(near(-step), 1, 0) + jnp.where(near(step), 1, 0)

        @pl.when(late & (count > 0))
        def _():
            pl.semaphore_wait(z_met.at[n], count)

    pass_on(0, 2)
    for n in range(FIRST_LATE - 1):

        @pl.when((n < z) & (z < FIRST_LATE))
        def _():
            tell(3, n)

    for copy in own[2:]:
        copy.wait()
    lanes = lax.broadcasted_iota(jnp.int32, (GROUP, SEG), 1)
    valid = jnp.where((lanes < TOK) & (z * TOK + lanes < IMG_TOK), 0.0, NEG)
    first_slot = jnp.where(even, 2 * y, 2 * SIDE * x)
    step = jnp.where(even, 2 * SIDE, 2)

    @pl.loop(0, LINE)
    def _(n):
        place = lax.div(n, 2)
        chip = jnp.where(even, x * SIDE + place, place * SIDE + y)
        for r in range(2):
            request = 4 * chip + 2 * lax.rem(n, 2) + r
            cited = count_ref[request]
            named = [jnp.where(j < cited, slot_ref[lists_ref[j, request]], -1) for j in range(LISTS)]
            for m in range(LINE):
                slot = first_slot + step * (m // 2) + m % 2
                hit = jnp.int32(0)
                for name in named:
                    hit = hit + jnp.where(name == slot, 1, 0)
                level = jnp.where(hit > 0, 0.0, NEG)
                bias[n, r * GROUP : (r + 1) * GROUP, m * SEG : (m + 1) * SEG] = valid + level

    told(0, 2)
    pass_on(1, 4)

    others = pl.ds(0, LINE - 1)
    lane = lax.broadcasted_iota(jnp.int32, (LINE, GROUP, HD), 2)

    def work(s):
        if s == 0:
            wait_bytes(q_buf.at[others, 0], q_recv.at[0])
            wait_bytes(kv_buf.at[0, others, 0, sent], kv_recv.at[0])
        else:
            if s == 1:
                wait_bytes(q_buf.at[others, later], q_recv.at[1])
            wait_bytes(kv_buf.at[s, others, :, sent], kv_recv.at[s + 1])
        queries = q_buf[:, s].reshape(LINE * ROWS, HD)
        keys = kv_buf[s, :, 0].reshape(LINE * SEG, HD)
        scores = lax.dot_general(
            queries, keys, (((1,), (1,)), ((), ())), preferred_element_type=jnp.float32
        )
        scores = scores * SCALE + bias[...].reshape(LINE * ROWS, LINE * SEG)
        peak = jnp.max(scores, axis=1, keepdims=True)
        weights = jnp.exp2(scores - peak)
        total = jnp.sum(weights, axis=1, keepdims=True)
        high = weights.astype(jnp.bfloat16)
        low = (weights - high.astype(jnp.float32)).astype(jnp.bfloat16)
        if s == 0:
            wait_bytes(kv_buf.at[0, others, 1, sent], kv_recv.at[1])
        values = kv_buf[s, :, 1].reshape(LINE * SEG, HD)
        weighted = jnp.dot(high, values, preferred_element_type=jnp.float32)
        weighted += jnp.dot(low, values, preferred_element_type=jnp.float32)
        home_out[s, :, :ROWS, :] = (weighted / total).reshape(LINE, ROWS, HD)
        size = (peak + jnp.log2(total)).reshape(LINE, 2, GROUP, 1)
        stat = jnp.where(lane == 0, size[:, 0], jnp.where(lane == 1, size[:, 1], 0.0))
        home_out[s, :, ROWS:, :] = stat
        place = SIDE * core + q_place
        for d in (2, 1, 3):
            there = lax.rem(q_place + d, SIDE)
            for c in range(2):
                to = device(jnp.where(even, x, there), jnp.where(even, there, y), c)
                send(home_out.at[s, 2 * there + c], home_in.at[s, place], (h_send, h_recv), s, to)
        send(home_out.at[s, 2 * q_place + 1 - core], home_in.at[s, place], (h_send, h_recv), s, other_core)
        home_in[s, place] = home_out[s, 2 * q_place + core]

    diagonal = lax.broadcasted_iota(jnp.int32, (GROUP, HD), 0) == lax.broadcasted_iota(jnp.int32, (GROUP, HD), 1)
    low_rows = lax.broadcasted_iota(jnp.int32, (GROUP, HD), 0) < GROUP // 2

    def spread(s):
        wait_bytes(home_in.at[s, others], h_recv.at[s])
        for c in range(2):
            mine = home_in[s, c * SIDE : (c + 1) * SIDE]
            sizes = mine[:, ROWS:, :]
            largest = jnp.max(sizes, axis=0)
            share = jnp.exp2(sizes - largest[None])
            total = jnp.sum(share, axis=0)
            share = share / total[None]
            size = largest + jnp.log2(total)
            results, logs = [], []
            for r in range(2):
                at = r * GROUP
                results.append(jnp.sum(mine[:, at : at + GROUP, :] * share[:, :, r : r + 1], axis=0))
                logs.append(jnp.broadcast_to(size[:, r : r + 1], (GROUP, HD)))
            for h in range(2):
                there = 4 * PAIRS[s] + 2 * c + h
                tiles = []
                for a, b in (results, logs):
                    if h == 0:
                        tiles.append(jnp.where(low_rows, a, pltpu.roll(b, GROUP // 2, 0)))
                    else:
                        tiles.append(jnp.where(low_rows, pltpu.roll(a, GROUP // 2, 0), b))
                z_out[there, :GROUP, :] = tiles[0]
                z_out[there, GROUP:, :] = jnp.sum(jnp.where(diagonal, tiles[1], 0.0), axis=0, keepdims=True)

                @pl.when(z != there)
                def _():
                    pltpu.make_async_remote_copy(
                        src_ref=z_out.at[there], dst_ref=z_in.at[z], send_sem=z_send, recv_sem=z_recv,
                        device_id=device(x, y, core, there), device_id_type=MESH,
                    ).start()

                @pl.when(z == there)
                def _():
                    z_in[z] = z_out[there]

    work(0)

    send_kv(3, 2, both)
    work(1)
    send_kv(4, 3, both)
    told(1, 4)
    for n in range(FIRST_LATE):

        @pl.when(late)
        def _():
            tell(2, n)

    @pl.when(z < FIRST_LATE - 1)
    def _():
        pl.semaphore_wait(z_met.at[3], FIRST_LATE - 1 - z)

    spread(0)
    work(2)
    spread(1)
    work(3)

    @pl.when(z < FIRST_LATE)
    def _():
        pl.semaphore_wait(z_met.at[2], NZ - FIRST_LATE)

    spread(2)
    spread(3)

    wait_bytes(z_in.at[pl.ds(0, NZ - 1)], z_recv)
    sizes = jnp.sum(jnp.where(diagonal[None], z_in[:, GROUP:, :], 0.0), axis=2, keepdims=True)
    largest = jnp.max(sizes, axis=0)
    share = jnp.exp2(sizes - largest[None])
    out_ref[...] = jnp.sum(z_in[:, :GROUP, :] * share, axis=0) / jnp.sum(share, axis=0)

    wait_bytes(q_buf.at[others, 0], q_send.at[0])
    wait_bytes(q_buf.at[others, later], q_send.at[1])
    for i in range(2):
        wait_bytes(kv_buf.at[0, others, i, sent], kv_send.at[i])
    for s in range(1, STAGES):
        wait_bytes(kv_buf.at[s, others, :, sent], kv_send.at[s + 1])
    for s in range(STAGES):
        wait_bytes(home_in.at[s, others], h_send.at[s])
    wait_bytes(z_in.at[pl.ds(0, NZ - 1)], z_send)


def per_device(queries, image_cache, image_lists, cited_count, image_slot):
    home = (STAGES, LINE, ROWS + GROUP, HD)
    along_z = (NZ, GROUP + 1, HD)
    result = pl.pallas_call(
        kernel,
        name="attend",
        out_shape=pltpu.VMEM((GROUP, HD), jnp.float32),
        in_specs=[pl.BlockSpec(memory_space=pl.ANY)] * 5,
        out_specs=pl.BlockSpec(memory_space=pltpu.VMEM),
        scratch_shapes=[
            pltpu.VMEM(queries.shape, jnp.bfloat16),
            pltpu.VMEM(image_cache.shape, jnp.bfloat16),
            pltpu.SMEM((LISTS, REQS), jnp.int32),
            pltpu.SMEM((REQS,), jnp.int32),
            pltpu.SMEM((IMAGES,), jnp.int32),
            pltpu.VMEM((2, STAGES, ROWS, HD), jnp.bfloat16),
            pltpu.VMEM((KVH, 2, TOK_SENT, HD), jnp.bfloat16),
            pltpu.VMEM((LINE, STAGES, ROWS, HD), jnp.bfloat16),
            pltpu.VMEM((STAGES, LINE, 2, SEG, HD), jnp.bfloat16),
            pltpu.VMEM((LINE, ROWS, LINE * SEG), jnp.float32),
            pltpu.VMEM(home, jnp.float32),
            pltpu.VMEM(home, jnp.float32),
            pltpu.VMEM(along_z, jnp.float32),
            pltpu.VMEM(along_z, jnp.float32),
            pltpu.SemaphoreType.DMA((5,)),
            pltpu.SemaphoreType.DMA((2,)),
            pltpu.SemaphoreType.DMA((2,)),
            pltpu.SemaphoreType.DMA((STAGES + 1,)),
            pltpu.SemaphoreType.DMA((STAGES + 1,)),
            pltpu.SemaphoreType.DMA((STAGES,)),
            pltpu.SemaphoreType.DMA((STAGES,)),
            pltpu.SemaphoreType.DMA,
            pltpu.SemaphoreType.DMA,
            pltpu.SemaphoreType.REGULAR((4,)),
        ],
        compiler_params=pltpu.CompilerParams(
            collective_id=0, has_side_effects=True, vmem_limit_bytes=60 * 2**20
        ),
    )(queries, image_cache, image_lists.T, cited_count, image_slot)
    return result.reshape(2, GROUP // 2 * HD)


def solution(mesh):
    return jax.shard_map(
        per_device,
        mesh=mesh,
        in_specs=(P("req", None), P("req", "tp", None), P(), P(), P()),
        out_specs=P("req", "tp"),
        check_vma=False,
    )
```

```python
import math

import jax
import jax.numpy as jnp
from jax import lax
from jax.experimental import pallas as pl
from jax.experimental.pallas import tpu as pltpu
from jax.sharding import PartitionSpec as P

KVH = 8
GROUP = 8
HD = 128
IMG_TOK = 1601
LISTS = 4
SIDE = 4
NZ = 16
REQS = 64
IMAGES = 32
TOK = 104
TOK_SENT = 112
SEG = 128
LINE = 2 * SIDE
ROWS = 16
STAGES = (0, 1, 2, 3, 6, 7, 4, 5)
AHEAD = 3
NEG = -1e30
SCALE = math.log2(math.e) / math.sqrt(HD)
MESH = pl.DeviceIdType.MESH
FIRST_LATE = NZ // 2
GREETED = tuple(min(n, 8) if n < 12 else 7 if n == 12 else 6 for n in range(NZ))


def wait_bytes(ref, sem):
    pltpu.make_async_copy(ref, ref, sem).wait()


def kernel(
    q_hbm, cache_hbm, lists_hbm, count_hbm, slot_hbm, out_ref,
    q_ref, cache_ref, lists_ref, count_ref, slot_ref,
    q_own, q_buf, kv_buf, bias, home_out, home_in, z_out, z_in,
    own_sem, q_send, q_recv, kv_send, kv_recv, h_send, h_recv, z_send, z_recv, z_met,
):
    req = lax.axis_index("req")
    z = lax.axis_index("tp")
    core = lax.rem(req, 2)
    x = lax.div(req, 2 * SIDE)
    y = lax.rem(lax.div(req, 2), SIDE)
    even = core == 0

    def device(x_, y_, c_, z_=z):
        return ((x_ * SIDE + y_) * 2 + c_, z_)

    def along_x(d, c_):
        return device(lax.rem(x + d, SIDE), y, c_)

    def along_y(d, c_):
        return device(x, lax.rem(y + d, SIDE), c_)

    def along_z(d):
        return device(x, y, core, lax.rem(z + d + NZ, NZ))

    other_core = device(x, y, 1 - core)
    kv_place = jnp.where(even, x, y)
    q_place = jnp.where(even, y, x)

    barrier = pltpu.get_barrier_semaphore()
    met = [line(d, c_) for d in (2, 1, 3) for line in (along_x, along_y) for c_ in range(2)]
    met += [other_core]
    for there in met:
        pl.semaphore_signal(barrier, inc=1, device_id=there, device_id_type=MESH)
    late = z >= FIRST_LATE

    def near(d):
        return late & (z + d >= FIRST_LATE) & (z + d < NZ)

    for d in (-2, -1, 1, 2):

        @pl.when(near(d))
        def _():
            pl.semaphore_signal(barrier, inc=1, device_id=along_z(d), device_id_type=MESH)

    for n in range(NZ - 1, 0, -1):

        @pl.when(z < GREETED[n])
        def _():
            there = device(x, y, core, n)
            pl.semaphore_signal(barrier, inc=1, device_id=there, device_id_type=MESH)

    own = [
        pltpu.make_async_copy(src, dst, own_sem.at[i])
        for i, (src, dst) in enumerate(
            (
                (q_hbm, q_ref),
                (cache_hbm, cache_ref),
                (lists_hbm, lists_ref),
                (count_hbm, count_ref),
                (slot_hbm, slot_ref),
            )
        )
    ]
    for copy in own:
        copy.start()

    own[0].wait()
    for s, head in enumerate(STAGES):
        first = head * GROUP * HD
        mine = q_ref[:, first : first + GROUP * HD].astype(jnp.float32)
        rows = [mine[r : r + 1, g * HD : (g + 1) * HD] for r in range(2) for g in range(GROUP)]
        q_own[s] = jnp.concatenate(rows, axis=0).astype(jnp.bfloat16)
    q_buf[2 * q_place + core] = q_own[...]

    own[1].wait()
    tail = jnp.zeros((TOK_SENT - TOK, HD), jnp.bfloat16)
    pad = jnp.zeros((SEG - TOK_SENT, HD), jnp.bfloat16)
    for s, head in enumerate(STAGES):
        for i in range(2):
            first = (i * KVH + head) * HD
            block = jnp.concatenate([cache_ref[0, :, first : first + HD], tail], axis=0)
            kv_buf[s, kv_place, i, :TOK_SENT, :] = block
            for n in range(SIDE):
                kv_buf[s, n, i, TOK_SENT:, :] = pad

    greeted = jnp.int32(len(met))
    for d in (-2, -1, 1, 2):
        greeted = greeted + jnp.where(near(d), 1, 0)
    for n in range(1, NZ):
        greeted = greeted + jnp.where(z == n, GREETED[n], 0)
    pl.semaphore_wait(barrier, greeted)

    def send(src, dst, sems, n, there):
        send_sem, recv_sem = sems
        pltpu.make_async_remote_copy(
            src_ref=src, dst_ref=dst, send_sem=send_sem.at[n], recv_sem=recv_sem.at[n],
            device_id=there, device_id_type=MESH,
        ).start()

    sent = pl.ds(0, TOK_SENT)

    def send_kv(n, s, part):
        for d in (2, 1, 3):
            place = lax.rem(kv_place + d, SIDE)
            there = device(jnp.where(even, place, x), jnp.where(even, y, place), core)
            block = kv_buf.at[s, kv_place, part, sent]
            send(block, block, (kv_send, kv_recv), n, there)

    def send_q(n, stages):
        for d in (2, 1, 3):
            for c, line, place in ((0, along_y, y), (1, along_x, x)):
                src, dst = q_own.at[stages], q_buf.at[2 * place + core, stages]
                send(src, dst, (q_send, q_recv), n, line(d, c))
        src, dst = q_own.at[stages], q_buf.at[2 * kv_place + core, stages]
        send(src, dst, (q_send, q_recv), n, other_core)

    both = slice(None)
    soon, later = pl.ds(0, 2), pl.ds(2, KVH - 2)
    send_q(0, soon)
    send_kv(0, 0, 0)
    send_kv(1, 0, 1)
    send_kv(2, 1, both)
    send_q(1, later)
    for s in range(2, AHEAD):
        send_kv(s + 1, s, both)

    def tell(n, there):
        pl.semaphore_signal(z_met.at[n], inc=1, device_id=device(x, y, core, there), device_id_type=MESH)

    def pass_on(n, step):
        for d in (-step, step):

            @pl.when(near(d))
            def _():
                tell(n, z + d)

    def told(n, step):
        count = jnp.where(near(-step), 1, 0) + jnp.where(near(step), 1, 0)

        @pl.when(late & (count > 0))
        def _():
            pl.semaphore_wait(z_met.at[n], count)

    pass_on(0, 2)
    for n in range(FIRST_LATE - 1):

        @pl.when((n < z) & (z < FIRST_LATE))
        def _():
            tell(3, n)

    for copy in own[2:]:
        copy.wait()
    lanes = lax.broadcasted_iota(jnp.int32, (GROUP, SEG), 1)
    valid = jnp.where((lanes < TOK) & (z * TOK + lanes < IMG_TOK), 0.0, NEG)
    first_slot = jnp.where(even, 2 * y, 2 * SIDE * x + 1)
    step = jnp.where(even, 2 * SIDE, 2)

    @pl.loop(0, LINE)
    def _(n):
        place = lax.div(n, 2)
        chip = jnp.where(even, x * SIDE + place, place * SIDE + y)
        for r in range(2):
            request = 4 * chip + 2 * lax.rem(n, 2) + r
            cited = count_ref[request]
            named = [jnp.where(j < cited, slot_ref[lists_ref[j, request]], -1) for j in range(LISTS)]
            for m in range(SIDE):
                slot = first_slot + step * m
                hit = jnp.int32(0)
                for name in named:
                    hit = hit + jnp.where(name == slot, 1, 0)
                level = jnp.where(hit > 0, 0.0, NEG)
                bias[n, r * GROUP : (r + 1) * GROUP, m * SEG : (m + 1) * SEG] = valid + level

    told(0, 2)
    pass_on(1, 4)

    others, line_others = pl.ds(0, LINE - 1), pl.ds(0, SIDE - 1)
    iota = [lax.broadcasted_iota(jnp.int32, (1, 2, GROUP, HD), i) for i in range(4)]
    in_row = iota[3] == iota[1] * GROUP + iota[2]

    def work(s):
        if s == 0:
            wait_bytes(q_buf.at[others, soon], q_recv.at[0])
            wait_bytes(kv_buf.at[0, line_others, 0, sent], kv_recv.at[0])
        else:
            if s == 2:
                wait_bytes(q_buf.at[others, later], q_recv.at[1])
            wait_bytes(kv_buf.at[s, line_others, :, sent], kv_recv.at[s + 1])
        queries = q_buf[:, s].reshape(LINE * ROWS, HD)
        keys = kv_buf[s, :, 0].reshape(SIDE * SEG, HD)
        scores = lax.dot_general(
            queries, keys, (((1,), (1,)), ((), ())), preferred_element_type=jnp.float32
        )
        scores = scores * SCALE + bias[...].reshape(LINE * ROWS, SIDE * SEG)
        peak = jnp.max(scores, axis=1, keepdims=True)
        weights = jnp.exp2(scores - peak)
        total = jnp.sum(weights, axis=1, keepdims=True)
        high = weights.astype(jnp.bfloat16)
        low = (weights - high.astype(jnp.float32)).astype(jnp.bfloat16)
        if s == 0:
            wait_bytes(kv_buf.at[0, line_others, 1, sent], kv_recv.at[1])
        values = kv_buf[s, :, 1].reshape(SIDE * SEG, HD)
        weighted = jnp.dot(high, values, preferred_element_type=jnp.float32)
        weighted += jnp.dot(low, values, preferred_element_type=jnp.float32)
        home_out[s, :, :ROWS, :] = (weighted / total).reshape(LINE, ROWS, HD)
        size = (peak + jnp.log2(total)).reshape(LINE, 2, GROUP, 1)
        row = jnp.sum(jnp.where(in_row, size, 0.0), axis=2, keepdims=True)
        home_out[s, :, ROWS:, :] = jnp.sum(row, axis=1)
        place = SIDE * core + q_place
        for d in (2, 1, 3):
            there = lax.rem(q_place + d, SIDE)
            for c in range(2):
                to = device(jnp.where(even, x, there), jnp.where(even, there, y), c)
                send(home_out.at[s, 2 * there + c], home_in.at[s, place], (h_send, h_recv), s, to)
        send(home_out.at[s, 2 * q_place + 1 - core], home_in.at[s, place], (h_send, h_recv), s, other_core)
        home_in[s, place] = home_out[s, 2 * q_place + core]
        if s + AHEAD < KVH:
            send_kv(s + AHEAD + 1, s + AHEAD, both)

    diagonal = lax.broadcasted_iota(jnp.int32, (GROUP, HD), 0) == lax.broadcasted_iota(jnp.int32, (GROUP, HD), 1)
    low_rows = lax.broadcasted_iota(jnp.int32, (GROUP, HD), 0) < GROUP // 2

    def spread(s):
        wait_bytes(home_in.at[s, others], h_recv.at[s])
        row = home_in[s, :, ROWS:, :].reshape(LINE, 1, 1, HD)
        sizes = jnp.sum(jnp.where(in_row, row, 0.0), axis=3, keepdims=True)
        largest = jnp.max(sizes, axis=0)
        share = jnp.exp2(sizes - largest[None])
        total = jnp.sum(share, axis=0)
        share = share / total[None]
        size = largest + jnp.log2(total)
        results, logs = [], []
        for r in range(2):
            part = home_in[s, :, r * GROUP : (r + 1) * GROUP, :]
            results.append(jnp.sum(part * share[:, r], axis=0))
            logs.append(jnp.broadcast_to(size[r], (GROUP, HD)))
        for h in range(2):
            there = 2 * STAGES[s] + h
            tiles = []
            for a, b in (results, logs):
                if h == 0:
                    tiles.append(jnp.where(low_rows, a, pltpu.roll(b, GROUP // 2, 0)))
                else:
                    tiles.append(jnp.where(low_rows, pltpu.roll(a, GROUP // 2, 0), b))
            z_out[there, :GROUP, :] = tiles[0]
            z_out[there, GROUP:, :] = jnp.sum(jnp.where(diagonal, tiles[1], 0.0), axis=0, keepdims=True)

            @pl.when(z != there)
            def _():
                pltpu.make_async_remote_copy(
                    src_ref=z_out.at[there], dst_ref=z_in.at[z], send_sem=z_send, recv_sem=z_recv,
                    device_id=device(x, y, core, there), device_id_type=MESH,
                ).start()

            @pl.when(z == there)
            def _():
                z_in[z] = z_out[there]

    work(0)
    told(1, 4)
    for n in range(FIRST_LATE):

        @pl.when(late)
        def _():
            tell(2, n)

    for s in range(1, 3):
        work(s)

    @pl.when(z < FIRST_LATE - 1)
    def _():
        pl.semaphore_wait(z_met.at[3], FIRST_LATE - 1 - z)

    spread(0)
    for s in range(1, KVH):
        if s + 3 - 1 < KVH:
            work(s + 3 - 1)
        if STAGES[s] * 2 >= FIRST_LATE and STAGES[s - 1] * 2 < FIRST_LATE:

            @pl.when(z < FIRST_LATE)
            def _():
                pl.semaphore_wait(z_met.at[2], NZ - FIRST_LATE)

        spread(s)

    wait_bytes(z_in.at[pl.ds(0, NZ - 1)], z_recv)
    sizes = jnp.sum(jnp.where(diagonal[None], z_in[:, GROUP:, :], 0.0), axis=2, keepdims=True)
    largest = jnp.max(sizes, axis=0)
    share = jnp.exp2(sizes - largest[None])
    result = jnp.sum(z_in[:, :GROUP, :] * share, axis=0) / jnp.sum(share, axis=0)
    for r in range(2):
        for g in range(GROUP // 2):
            at = r * (GROUP // 2) + g
            out_ref[r : r + 1, g * HD : (g + 1) * HD] = result[at : at + 1]

    wait_bytes(q_buf.at[others, soon], q_send.at[0])
    wait_bytes(q_buf.at[others, later], q_send.at[1])
    for i in range(2):
        wait_bytes(kv_buf.at[0, line_others, i, sent], kv_send.at[i])
    for s in range(1, KVH):
        wait_bytes(kv_buf.at[s, line_others, :, sent], kv_send.at[s + 1])
    for s in range(KVH):
        wait_bytes(home_in.at[s, others], h_send.at[s])
    wait_bytes(z_in.at[pl.ds(0, NZ - 1)], z_send)


def per_device(queries, image_cache, image_lists, cited_count, image_slot):
    home = (KVH, LINE, ROWS + 1, HD)
    along_z = (NZ, GROUP + 1, HD)
    return pl.pallas_call(
        kernel,
        name="attend",
        out_shape=pltpu.VMEM((2, GROUP // 2 * HD), jnp.float32),
        in_specs=[pl.BlockSpec(memory_space=pl.ANY)] * 5,
        out_specs=pl.BlockSpec(memory_space=pltpu.VMEM),
        scratch_shapes=[
            pltpu.VMEM(queries.shape, jnp.bfloat16),
            pltpu.VMEM(image_cache.shape, jnp.bfloat16),
            pltpu.SMEM((LISTS, REQS), jnp.int32),
            pltpu.SMEM((REQS,), jnp.int32),
            pltpu.SMEM((IMAGES,), jnp.int32),
            pltpu.VMEM((KVH, ROWS, HD), jnp.bfloat16),
            pltpu.VMEM((LINE, KVH, ROWS, HD), jnp.bfloat16),
            pltpu.VMEM((KVH, SIDE, 2, SEG, HD), jnp.bfloat16),
            pltpu.VMEM((LINE, ROWS, SIDE * SEG), jnp.float32),
            pltpu.VMEM(home, jnp.float32),
            pltpu.VMEM(home, jnp.float32),
            pltpu.VMEM(along_z, jnp.float32),
            pltpu.VMEM(along_z, jnp.float32),
            pltpu.SemaphoreType.DMA((5,)),
            pltpu.SemaphoreType.DMA((2,)),
            pltpu.SemaphoreType.DMA((2,)),
            pltpu.SemaphoreType.DMA((KVH + 1,)),
            pltpu.SemaphoreType.DMA((KVH + 1,)),
            pltpu.SemaphoreType.DMA((KVH,)),
            pltpu.SemaphoreType.DMA((KVH,)),
            pltpu.SemaphoreType.DMA,
            pltpu.SemaphoreType.DMA,
            pltpu.SemaphoreType.REGULAR((4,)),
        ],
        compiler_params=pltpu.CompilerParams(
            collective_id=0, has_side_effects=True, vmem_limit_bytes=60 * 2**20
        ),
    )(queries, image_cache, image_lists.T, cited_count, image_slot)


def solution(mesh):
    return jax.shard_map(
        per_device,
        mesh=mesh,
        in_specs=(P("req", None), P("req", "tp", None), P(), P(), P()),
        out_specs=P("req", "tp"),
        check_vma=False,
    )
```

```python
import math

import jax
import jax.numpy as jnp
from jax import lax
from jax.experimental import pallas as pl
from jax.experimental.pallas import tpu as pltpu
from jax.sharding import PartitionSpec as P

KVH = 8
GROUP = 8
HD = 128
IMG_TOK = 1601
LISTS = 4
SIDE = 4
NZ = 16
REQS = 64
IMAGES = 32
TOK = 104
LINE = 2 * SIDE
ROWS = 16
STAGES = (0, 1, 2, 3, 6, 7, 4, 5)
NEG = -1e30
SCALE = math.log2(math.e) / math.sqrt(HD)
MESH = pl.DeviceIdType.MESH
FIRST_LATE = NZ // 2
GREETED = tuple(min(n, 8) if n < 12 else 7 if n == 12 else 6 for n in range(NZ))


def wait_bytes(ref, sem):
    pltpu.make_async_copy(ref, ref, sem).wait()


def kernel(
    q_hbm, cache_hbm, lists_hbm, count_hbm, slot_hbm, out_ref,
    q_ref, cache_ref, lists_ref, count_ref, slot_ref,
    q_own, q_buf, kv_buf, bias, home_out, home_in, z_out, z_in,
    own_sem, q_send, q_recv, kv_send, kv_recv, h_send, h_recv, z_send, z_recv, z_met,
):
    req = lax.axis_index("req")
    z = lax.axis_index("tp")
    core = lax.rem(req, 2)
    x = lax.div(req, 2 * SIDE)
    y = lax.rem(lax.div(req, 2), SIDE)
    even = core == 0

    def device(x_, y_, c_, z_=z):
        return ((x_ * SIDE + y_) * 2 + c_, z_)

    def along_x(d, c_):
        return device(lax.rem(x + d, SIDE), y, c_)

    def along_y(d, c_):
        return device(x, lax.rem(y + d, SIDE), c_)

    def along_z(d):
        return device(x, y, core, lax.rem(z + d + NZ, NZ))

    other_core = device(x, y, 1 - core)
    kv_place = jnp.where(even, x, y)
    q_place = jnp.where(even, y, x)

    barrier = pltpu.get_barrier_semaphore()
    met = [line(d, c_) for d in (2, 1, 3) for line in (along_x, along_y) for c_ in range(2)]
    met += [other_core]
    for there in met:
        pl.semaphore_signal(barrier, inc=1, device_id=there, device_id_type=MESH)
    late = z >= FIRST_LATE

    def near(d):
        return late & (z + d >= FIRST_LATE) & (z + d < NZ)

    for d in (-2, -1, 1, 2):

        @pl.when(near(d))
        def _():
            pl.semaphore_signal(barrier, inc=1, device_id=along_z(d), device_id_type=MESH)

    for n in range(NZ - 1, 0, -1):

        @pl.when(z < GREETED[n])
        def _():
            there = device(x, y, core, n)
            pl.semaphore_signal(barrier, inc=1, device_id=there, device_id_type=MESH)

    own = [
        pltpu.make_async_copy(src, dst, own_sem.at[i])
        for i, (src, dst) in enumerate(
            (
                (q_hbm, q_ref),
                (cache_hbm, cache_ref),
                (lists_hbm, lists_ref),
                (count_hbm, count_ref),
                (slot_hbm, slot_ref),
            )
        )
    ]
    for copy in own:
        copy.start()

    own[0].wait()
    for s, head in enumerate(STAGES):
        first = head * GROUP * HD
        mine = q_ref[:, first : first + GROUP * HD].astype(jnp.float32)
        rows = [mine[r : r + 1, g * HD : (g + 1) * HD] for r in range(2) for g in range(GROUP)]
        q_own[s] = jnp.concatenate(rows, axis=0).astype(jnp.bfloat16)
    q_buf[2 * q_place + core] = q_own[...]

    own[1].wait()
    for s, head in enumerate(STAGES):
        for i in range(2):
            first = (i * KVH + head) * HD
            kv_buf[s, kv_place, i] = cache_ref[0, :, first : first + HD]

    greeted = jnp.int32(len(met))
    for d in (-2, -1, 1, 2):
        greeted = greeted + jnp.where(near(d), 1, 0)
    for n in range(1, NZ):
        greeted = greeted + jnp.where(z == n, GREETED[n], 0)
    pl.semaphore_wait(barrier, greeted)

    def send(src, dst, sems, n, there):
        send_sem, recv_sem = sems
        pltpu.make_async_remote_copy(
            src_ref=src, dst_ref=dst, send_sem=send_sem.at[n], recv_sem=recv_sem.at[n],
            device_id=there, device_id_type=MESH,
        ).start()


    def send_kv(n, s, part):
        for d in (2, 1, 3):
            place = lax.rem(kv_place + d, SIDE)
            there = device(jnp.where(even, place, x), jnp.where(even, y, place), core)
            block = kv_buf.at[s, kv_place, part]
            send(block, block, (kv_send, kv_recv), n, there)

    def send_q(n, stages):
        for d in (2, 1, 3):
            for c, line, place in ((0, along_y, y), (1, along_x, x)):
                src, dst = q_own.at[stages], q_buf.at[2 * place + core, stages]
                send(src, dst, (q_send, q_recv), n, line(d, c))
        src, dst = q_own.at[stages], q_buf.at[2 * kv_place + core, stages]
        send(src, dst, (q_send, q_recv), n, other_core)

    both = slice(None)
    soon, later = pl.ds(0, 2), pl.ds(2, KVH - 2)
    send_q(0, soon)
    send_kv(0, 0, 0)
    send_kv(1, 0, 1)
    send_kv(2, 1, both)
    send_q(1, later)
    send_kv(3, 2, both)
    send_kv(4, 3, both)

    def tell(n, there):
        pl.semaphore_signal(z_met.at[n], inc=1, device_id=device(x, y, core, there), device_id_type=MESH)

    def pass_on(n, step):
        for d in (-step, step):

            @pl.when(near(d))
            def _():
                tell(n, z + d)

    def told(n, step):
        count = jnp.where(near(-step), 1, 0) + jnp.where(near(step), 1, 0)

        @pl.when(late & (count > 0))
        def _():
            pl.semaphore_wait(z_met.at[n], count)

    pass_on(0, 2)
    for n in range(FIRST_LATE - 1):

        @pl.when((n < z) & (z < FIRST_LATE))
        def _():
            tell(3, n)

    for copy in own[2:]:
        copy.wait()
    lanes = lax.broadcasted_iota(jnp.int32, (GROUP, SIDE * TOK), 1)
    image = sum(jnp.where(lanes >= m * TOK, 1, 0) for m in range(1, SIDE))
    valid = jnp.where(z * TOK + lanes - image * TOK < IMG_TOK, 0.0, NEG)
    first_slot = jnp.where(even, 2 * y, 2 * SIDE * x + 1)
    step = jnp.where(even, 2 * SIDE, 2)

    @pl.loop(0, LINE)
    def _(n):
        place = lax.div(n, 2)
        chip = jnp.where(even, x * SIDE + place, place * SIDE + y)
        for r in range(2):
            request = 4 * chip + 2 * lax.rem(n, 2) + r
            cited = count_ref[request]
            named = [jnp.where(j < cited, slot_ref[lists_ref[j, request]], -1) for j in range(LISTS)]
            level = valid
            for m in range(SIDE):
                slot = first_slot + step * m
                hit = jnp.int32(0)
                for name in named:
                    hit = hit + jnp.where(name == slot, 1, 0)
                level = level + jnp.where(image == m, jnp.where(hit > 0, 0.0, NEG), 0.0)
            bias[n, r * GROUP : (r + 1) * GROUP, :] = level

    told(0, 2)
    pass_on(1, 4)

    others, line_others = pl.ds(0, LINE - 1), pl.ds(0, SIDE - 1)
    iota = [lax.broadcasted_iota(jnp.int32, (1, 2, GROUP, HD), i) for i in range(4)]
    in_row = iota[3] == iota[1] * GROUP + iota[2]

    def work(s):
        if s == 0:
            wait_bytes(q_buf.at[others, soon], q_recv.at[0])
            wait_bytes(kv_buf.at[0, line_others, 0], kv_recv.at[0])
        else:
            if s == 2:
                wait_bytes(q_buf.at[others, later], q_recv.at[1])
            wait_bytes(kv_buf.at[s, line_others], kv_recv.at[s + 1])
        queries = q_buf[:, s].reshape(LINE * ROWS, HD)
        keys = kv_buf[s, :, 0].reshape(SIDE * TOK, HD)
        scores = lax.dot_general(
            queries, keys, (((1,), (1,)), ((), ())), preferred_element_type=jnp.float32
        )
        scores = scores * SCALE + bias[...].reshape(LINE * ROWS, SIDE * TOK)
        peak = jnp.max(scores, axis=1, keepdims=True)
        weights = jnp.exp2(scores - peak)
        total = jnp.sum(weights, axis=1, keepdims=True)
        high = weights.astype(jnp.bfloat16)
        low = (weights - high.astype(jnp.float32)).astype(jnp.bfloat16)
        if s == 0:
            wait_bytes(kv_buf.at[0, line_others, 1], kv_recv.at[1])
        values = kv_buf[s, :, 1].reshape(SIDE * TOK, HD)
        weighted = jnp.dot(high, values, preferred_element_type=jnp.float32)
        weighted += jnp.dot(low, values, preferred_element_type=jnp.float32)
        home_out[s, :, :ROWS, :] = (weighted / total).reshape(LINE, ROWS, HD)
        size = (peak + jnp.log2(total)).reshape(LINE, 2, GROUP, 1)
        row = jnp.sum(jnp.where(in_row, size, 0.0), axis=2, keepdims=True)
        home_out[s, :, ROWS:, :] = jnp.sum(row, axis=1)
        place = SIDE * core + q_place
        for d in (2, 1, 3):
            there = lax.rem(q_place + d, SIDE)
            for c in range(2):
                to = device(jnp.where(even, x, there), jnp.where(even, there, y), c)
                send(home_out.at[s, 2 * there + c], home_in.at[s, place], (h_send, h_recv), s, to)
        send(home_out.at[s, 2 * q_place + 1 - core], home_in.at[s, place], (h_send, h_recv), s, other_core)
        home_in[s, place] = home_out[s, 2 * q_place + core]

    diagonal = lax.broadcasted_iota(jnp.int32, (GROUP, HD), 0) == lax.broadcasted_iota(jnp.int32, (GROUP, HD), 1)
    low_rows = lax.broadcasted_iota(jnp.int32, (GROUP, HD), 0) < GROUP // 2

    def spread(s):
        wait_bytes(home_in.at[s, others], h_recv.at[s])
        row = home_in[s, :, ROWS:, :].reshape(LINE, 1, 1, HD)
        sizes = jnp.sum(jnp.where(in_row, row, 0.0), axis=3, keepdims=True)
        largest = jnp.max(sizes, axis=0)
        share = jnp.exp2(sizes - largest[None])
        total = jnp.sum(share, axis=0)
        share = share / total[None]
        size = largest + jnp.log2(total)
        results, logs = [], []
        for r in range(2):
            part = home_in[s, :, r * GROUP : (r + 1) * GROUP, :]
            results.append(jnp.sum(part * share[:, r], axis=0))
            logs.append(jnp.broadcast_to(size[r], (GROUP, HD)))
        for h in range(2):
            there = 2 * STAGES[s] + h
            tiles = []
            for a, b in (results, logs):
                if h == 0:
                    tiles.append(jnp.where(low_rows, a, pltpu.roll(b, GROUP // 2, 0)))
                else:
                    tiles.append(jnp.where(low_rows, pltpu.roll(a, GROUP // 2, 0), b))
            z_out[there, :GROUP, :] = tiles[0]
            z_out[there, GROUP:, :] = jnp.sum(jnp.where(diagonal, tiles[1], 0.0), axis=0, keepdims=True)

            @pl.when(z != there)
            def _():
                pltpu.make_async_remote_copy(
                    src_ref=z_out.at[there], dst_ref=z_in.at[z], send_sem=z_send, recv_sem=z_recv,
                    device_id=device(x, y, core, there), device_id_type=MESH,
                ).start()

            @pl.when(z == there)
            def _():
                z_in[z] = z_out[there]

    work(0)
    send_kv(5, 4, both)
    told(1, 4)
    for n in range(FIRST_LATE):

        @pl.when(late)
        def _():
            tell(2, n)

    work(1)
    send_kv(6, 5, both)
    work(2)
    send_kv(7, 6, both)
    @pl.when(z < FIRST_LATE - 1)
    def _():
        pl.semaphore_wait(z_met.at[3], FIRST_LATE - 1 - z)

    spread(0)
    work(3)
    send_kv(8, 7, both)
    spread(1)
    work(4)
    spread(2)
    work(5)
    spread(3)
    work(6)
    work(7)
    @pl.when(z < FIRST_LATE)
    def _():
        pl.semaphore_wait(z_met.at[2], NZ - FIRST_LATE)

    spread(4)
    spread(5)
    spread(6)
    spread(7)

    wait_bytes(z_in.at[pl.ds(0, NZ - 1)], z_recv)
    sizes = jnp.sum(jnp.where(diagonal[None], z_in[:, GROUP:, :], 0.0), axis=2, keepdims=True)
    largest = jnp.max(sizes, axis=0)
    share = jnp.exp2(sizes - largest[None])
    result = jnp.sum(z_in[:, :GROUP, :] * share, axis=0) / jnp.sum(share, axis=0)
    for r in range(2):
        for g in range(GROUP // 2):
            at = r * (GROUP // 2) + g
            out_ref[r : r + 1, g * HD : (g + 1) * HD] = result[at : at + 1]

    wait_bytes(q_buf.at[others, soon], q_send.at[0])
    wait_bytes(q_buf.at[others, later], q_send.at[1])
    for i in range(2):
        wait_bytes(kv_buf.at[0, line_others, i], kv_send.at[i])
    for s in range(1, KVH):
        wait_bytes(kv_buf.at[s, line_others], kv_send.at[s + 1])
    for s in range(KVH):
        wait_bytes(home_in.at[s, others], h_send.at[s])
    wait_bytes(z_in.at[pl.ds(0, NZ - 1)], z_send)


def per_device(queries, image_cache, image_lists, cited_count, image_slot):
    home = (KVH, LINE, ROWS + 1, HD)
    along_z = (NZ, GROUP + 1, HD)
    return pl.pallas_call(
        kernel,
        name="attend",
        out_shape=pltpu.VMEM((2, GROUP // 2 * HD), jnp.float32),
        in_specs=[pl.BlockSpec(memory_space=pl.ANY)] * 5,
        out_specs=pl.BlockSpec(memory_space=pltpu.VMEM),
        scratch_shapes=[
            pltpu.VMEM(queries.shape, jnp.bfloat16),
            pltpu.VMEM(image_cache.shape, jnp.bfloat16),
            pltpu.SMEM((LISTS, REQS), jnp.int32),
            pltpu.SMEM((REQS,), jnp.int32),
            pltpu.SMEM((IMAGES,), jnp.int32),
            pltpu.VMEM((KVH, ROWS, HD), jnp.bfloat16),
            pltpu.VMEM((LINE, KVH, ROWS, HD), jnp.bfloat16),
            pltpu.VMEM((KVH, SIDE, 2, TOK, HD), jnp.bfloat16),
            pltpu.VMEM((LINE, ROWS, SIDE * TOK), jnp.float32),
            pltpu.VMEM(home, jnp.float32),
            pltpu.VMEM(home, jnp.float32),
            pltpu.VMEM(along_z, jnp.float32),
            pltpu.VMEM(along_z, jnp.float32),
            pltpu.SemaphoreType.DMA((5,)),
            pltpu.SemaphoreType.DMA((2,)),
            pltpu.SemaphoreType.DMA((2,)),
            pltpu.SemaphoreType.DMA((KVH + 1,)),
            pltpu.SemaphoreType.DMA((KVH + 1,)),
            pltpu.SemaphoreType.DMA((KVH,)),
            pltpu.SemaphoreType.DMA((KVH,)),
            pltpu.SemaphoreType.DMA,
            pltpu.SemaphoreType.DMA,
            pltpu.SemaphoreType.REGULAR((4,)),
        ],
        compiler_params=pltpu.CompilerParams(
            collective_id=0, has_side_effects=True, vmem_limit_bytes=60 * 2**20
        ),
    )(queries, image_cache, image_lists.T, cited_count, image_slot)


def solution(mesh):
    return jax.shard_map(
        per_device,
        mesh=mesh,
        in_specs=(P("req", None), P("req", "tp", None), P(), P(), P()),
        out_specs=P("req", "tp"),
        check_vma=False,
    )
```

```python
import math

import jax
import jax.numpy as jnp
from jax import lax
from jax.experimental import pallas as pl
from jax.experimental.pallas import tpu as pltpu
from jax.sharding import PartitionSpec as P

KVH = 8
GROUP = 8
HD = 128
IMG_TOK = 1601
LISTS = 4
SIDE = 4
NZ = 16
REQS = 64
IMAGES = 32
TOK = 104
LINE = 2 * SIDE
ROWS = 16
STAGES = (0, 1, 2, 3, 6, 7, 4, 5)
NEG = -1e30
SCALE = math.log2(math.e) / math.sqrt(HD)
MESH = pl.DeviceIdType.MESH
FIRST_LATE = NZ // 2
GREETED = tuple(min(n, 8) if n < 12 else 7 if n == 12 else 6 for n in range(NZ))


def wait_bytes(ref, sem):
    pltpu.make_async_copy(ref, ref, sem).wait()


def kernel(
    q_hbm, cache_hbm, lists_hbm, count_hbm, slot_hbm, out_ref,
    q_ref, cache_ref, lists_ref, count_ref, slot_ref,
    q_own, q_buf, kv_buf, bias, home_out, home_in, z_out, z_in,
    own_sem, q_send, q_recv, kv_send, kv_recv, h_send, h_recv, z_send, z_recv, z_met,
):
    req = lax.axis_index("req")
    z = lax.axis_index("tp")
    core = lax.rem(req, 2)
    x = lax.div(req, 2 * SIDE)
    y = lax.rem(lax.div(req, 2), SIDE)
    even = core == 0

    def device(x_, y_, c_, z_=z):
        return ((x_ * SIDE + y_) * 2 + c_, z_)

    def along_x(d, c_):
        return device(lax.rem(x + d, SIDE), y, c_)

    def along_y(d, c_):
        return device(x, lax.rem(y + d, SIDE), c_)

    def along_z(d):
        return device(x, y, core, lax.rem(z + d + NZ, NZ))

    other_core = device(x, y, 1 - core)
    kv_place = jnp.where(even, x, y)
    q_place = jnp.where(even, y, x)

    barrier = pltpu.get_barrier_semaphore()
    met = [line(d, c_) for d in (2, 1, 3) for line in (along_x, along_y) for c_ in range(2)]
    met += [other_core]
    for there in met:
        pl.semaphore_signal(barrier, inc=1, device_id=there, device_id_type=MESH)
    own = [
        pltpu.make_async_copy(src, dst, own_sem.at[i])
        for i, (src, dst) in enumerate(
            (
                (q_hbm, q_ref),
                (cache_hbm, cache_ref),
                (lists_hbm, lists_ref),
                (count_hbm, count_ref),
                (slot_hbm, slot_ref),
            )
        )
    ]
    for copy in own:
        copy.start()

    late = z >= FIRST_LATE

    def near(d):
        return late & (z + d >= FIRST_LATE) & (z + d < NZ)

    for d in (-2, -1, 1, 2):

        @pl.when(near(d))
        def _():
            pl.semaphore_signal(barrier, inc=1, device_id=along_z(d), device_id_type=MESH)

    for n in range(NZ - 1, 0, -1):

        @pl.when(z < GREETED[n])
        def _():
            there = device(x, y, core, n)
            pl.semaphore_signal(barrier, inc=1, device_id=there, device_id_type=MESH)

    own[0].wait()
    for s, head in enumerate(STAGES):
        first = head * GROUP * HD
        mine = q_ref[:, first : first + GROUP * HD].astype(jnp.float32)
        rows = [mine[r : r + 1, g * HD : (g + 1) * HD] for r in range(2) for g in range(GROUP)]
        q_own[s] = jnp.concatenate(rows, axis=0).astype(jnp.bfloat16)
    q_buf[2 * q_place + core] = q_own[...]

    own[1].wait()
    for s, head in enumerate(STAGES):
        for i in range(2):
            first = (i * KVH + head) * HD
            kv_buf[s, kv_place, i] = cache_ref[0, :, first : first + HD]

    greeted = jnp.int32(len(met))
    for d in (-2, -1, 1, 2):
        greeted = greeted + jnp.where(near(d), 1, 0)
    for n in range(1, NZ):
        greeted = greeted + jnp.where(z == n, GREETED[n], 0)
    pl.semaphore_wait(barrier, greeted)

    def send(src, dst, sems, n, there):
        send_sem, recv_sem = sems
        pltpu.make_async_remote_copy(
            src_ref=src, dst_ref=dst, send_sem=send_sem.at[n], recv_sem=recv_sem.at[n],
            device_id=there, device_id_type=MESH,
        ).start()


    def send_kv(n, s, part):
        for d in (2, 1, 3):
            place = lax.rem(kv_place + d, SIDE)
            there = device(jnp.where(even, place, x), jnp.where(even, y, place), core)
            block = kv_buf.at[s, kv_place, part]
            send(block, block, (kv_send, kv_recv), n, there)

    def send_q(n, stages):
        for d in (2, 1, 3):
            for c, line, place in ((0, along_y, y), (1, along_x, x)):
                src, dst = q_own.at[stages], q_buf.at[2 * place + core, stages]
                send(src, dst, (q_send, q_recv), n, line(d, c))
        src, dst = q_own.at[stages], q_buf.at[2 * kv_place + core, stages]
        send(src, dst, (q_send, q_recv), n, other_core)

    both = slice(None)
    soon, later = pl.ds(0, 2), pl.ds(2, KVH - 2)
    send_q(0, soon)
    send_kv(0, 0, 0)
    send_kv(1, 0, 1)
    send_kv(2, 1, both)
    send_q(1, later)
    send_kv(3, 2, both)
    send_kv(4, 3, both)

    def tell(n, there):
        pl.semaphore_signal(z_met.at[n], inc=1, device_id=device(x, y, core, there), device_id_type=MESH)

    def pass_on(n, step):
        for d in (-step, step):

            @pl.when(near(d))
            def _():
                tell(n, z + d)

    def told(n, step):
        count = jnp.where(near(-step), 1, 0) + jnp.where(near(step), 1, 0)

        @pl.when(late & (count > 0))
        def _():
            pl.semaphore_wait(z_met.at[n], count)

    pass_on(0, 2)
    for n in range(FIRST_LATE - 1):

        @pl.when((n < z) & (z < FIRST_LATE))
        def _():
            tell(3, n)

    for copy in own[2:]:
        copy.wait()
    lanes = lax.broadcasted_iota(jnp.int32, (GROUP, SIDE * TOK), 1)
    image = sum(jnp.where(lanes >= m * TOK, 1, 0) for m in range(1, SIDE))
    valid = jnp.where(z * TOK + lanes - image * TOK < IMG_TOK, 0.0, NEG)
    first_slot = jnp.where(even, 2 * y, 2 * SIDE * x + 1)
    step = jnp.where(even, 2 * SIDE, 2)

    @pl.loop(0, LINE)
    def _(n):
        place = lax.div(n, 2)
        chip = jnp.where(even, x * SIDE + place, place * SIDE + y)
        for r in range(2):
            request = 4 * chip + 2 * lax.rem(n, 2) + r
            cited = count_ref[request]
            named = [jnp.where(j < cited, slot_ref[lists_ref[j, request]], -1) for j in range(LISTS)]
            level = valid
            for m in range(SIDE):
                slot = first_slot + step * m
                hit = jnp.int32(0)
                for name in named:
                    hit = hit + jnp.where(name == slot, 1, 0)
                level = level + jnp.where(image == m, jnp.where(hit > 0, 0.0, NEG), 0.0)
            bias[n, r * GROUP : (r + 1) * GROUP, :] = level

    told(0, 2)
    pass_on(1, 4)

    others, line_others = pl.ds(0, LINE - 1), pl.ds(0, SIDE - 1)
    iota = [lax.broadcasted_iota(jnp.int32, (1, 2, GROUP, HD), i) for i in range(4)]
    in_row = iota[3] == iota[1] * GROUP + iota[2]

    def work(s):
        if s == 0:
            wait_bytes(q_buf.at[others, soon], q_recv.at[0])
            wait_bytes(kv_buf.at[0, line_others, 0], kv_recv.at[0])
        else:
            if s == 2:
                wait_bytes(q_buf.at[others, later], q_recv.at[1])
            wait_bytes(kv_buf.at[s, line_others], kv_recv.at[s + 1])
        queries = q_buf[:, s].reshape(LINE * ROWS, HD)
        keys = kv_buf[s, :, 0].reshape(SIDE * TOK, HD)
        scores = lax.dot_general(
            queries, keys, (((1,), (1,)), ((), ())), preferred_element_type=jnp.float32
        )
        scores = scores * SCALE + bias[...].reshape(LINE * ROWS, SIDE * TOK)
        peak = jnp.max(scores, axis=1, keepdims=True)
        weights = jnp.exp2(scores - peak)
        total = jnp.sum(weights, axis=1, keepdims=True)
        high = weights.astype(jnp.bfloat16)
        low = (weights - high.astype(jnp.float32)).astype(jnp.bfloat16)
        if s == 0:
            wait_bytes(kv_buf.at[0, line_others, 1], kv_recv.at[1])
        values = kv_buf[s, :, 1].reshape(SIDE * TOK, HD)
        weighted = jnp.dot(high, values, preferred_element_type=jnp.float32)
        weighted += jnp.dot(low, values, preferred_element_type=jnp.float32)
        home_out[s, :, :ROWS, :] = (weighted / total).reshape(LINE, ROWS, HD)
        size = (peak + jnp.log2(total)).reshape(LINE, 2, GROUP, 1)
        row = jnp.sum(jnp.where(in_row, size, 0.0), axis=2, keepdims=True)
        home_out[s, :, ROWS:, :] = jnp.sum(row, axis=1)
        place = SIDE * core + q_place
        for d in (2, 1, 3):
            there = lax.rem(q_place + d, SIDE)
            for c in range(2):
                to = device(jnp.where(even, x, there), jnp.where(even, there, y), c)
                send(home_out.at[s, 2 * there + c], home_in.at[s, place], (h_send, h_recv), s, to)
        send(home_out.at[s, 2 * q_place + 1 - core], home_in.at[s, place], (h_send, h_recv), s, other_core)
        home_in[s, place] = home_out[s, 2 * q_place + core]

    diagonal = lax.broadcasted_iota(jnp.int32, (GROUP, HD), 0) == lax.broadcasted_iota(jnp.int32, (GROUP, HD), 1)
    low_rows = lax.broadcasted_iota(jnp.int32, (GROUP, HD), 0) < GROUP // 2

    def spread(s):
        wait_bytes(home_in.at[s, others], h_recv.at[s])
        row = home_in[s, :, ROWS:, :].reshape(LINE, 1, 1, HD)
        sizes = jnp.sum(jnp.where(in_row, row, 0.0), axis=3, keepdims=True)
        largest = jnp.max(sizes, axis=0)
        share = jnp.exp2(sizes - largest[None])
        total = jnp.sum(share, axis=0)
        share = share / total[None]
        size = largest + jnp.log2(total)
        results, logs = [], []
        for r in range(2):
            part = home_in[s, :, r * GROUP : (r + 1) * GROUP, :]
            results.append(jnp.sum(part * share[:, r], axis=0))
            logs.append(jnp.broadcast_to(size[r], (GROUP, HD)))
        for h in range(2):
            there = 2 * STAGES[s] + h
            tiles = []
            for a, b in (results, logs):
                if h == 0:
                    tiles.append(jnp.where(low_rows, a, pltpu.roll(b, GROUP // 2, 0)))
                else:
                    tiles.append(jnp.where(low_rows, pltpu.roll(a, GROUP // 2, 0), b))
            z_out[there, :GROUP, :] = tiles[0]
            z_out[there, GROUP:, :] = jnp.sum(jnp.where(diagonal, tiles[1], 0.0), axis=0, keepdims=True)

            @pl.when(z != there)
            def _():
                pltpu.make_async_remote_copy(
                    src_ref=z_out.at[there], dst_ref=z_in.at[z], send_sem=z_send, recv_sem=z_recv,
                    device_id=device(x, y, core, there), device_id_type=MESH,
                ).start()

            @pl.when(z == there)
            def _():
                z_in[z] = z_out[there]

    work(0)
    send_kv(5, 4, both)
    work(1)
    send_kv(6, 5, both)
    told(1, 4)
    for n in range(FIRST_LATE):

        @pl.when(late)
        def _():
            tell(2, n)

    work(2)
    send_kv(7, 6, both)
    @pl.when(z < FIRST_LATE - 1)
    def _():
        pl.semaphore_wait(z_met.at[3], FIRST_LATE - 1 - z)

    spread(0)
    work(3)
    send_kv(8, 7, both)
    spread(1)
    work(4)
    spread(2)
    work(5)
    spread(3)
    work(6)
    work(7)
    @pl.when(z < FIRST_LATE)
    def _():
        pl.semaphore_wait(z_met.at[2], NZ - FIRST_LATE)

    spread(4)
    spread(5)
    spread(6)
    spread(7)

    wait_bytes(q_buf.at[others, soon], q_send.at[0])
    wait_bytes(q_buf.at[others, later], q_send.at[1])
    for i in range(2):
        wait_bytes(kv_buf.at[0, line_others, i], kv_send.at[i])
    for s in range(1, KVH):
        wait_bytes(kv_buf.at[s, line_others], kv_send.at[s + 1])
    for s in range(KVH):
        wait_bytes(home_in.at[s, others], h_send.at[s])

    wait_bytes(z_in.at[pl.ds(0, NZ - 1)], z_recv)
    sizes = jnp.sum(jnp.where(diagonal[None], z_in[:, GROUP:, :], 0.0), axis=2, keepdims=True)
    largest = jnp.max(sizes, axis=0)
    share = jnp.exp2(sizes - largest[None])
    result = jnp.sum(z_in[:, :GROUP, :] * share, axis=0) / jnp.sum(share, axis=0)
    for r in range(2):
        for g in range(GROUP // 2):
            at = r * (GROUP // 2) + g
            out_ref[r : r + 1, g * HD : (g + 1) * HD] = result[at : at + 1]

    wait_bytes(z_in.at[pl.ds(0, NZ - 1)], z_send)


def per_device(queries, image_cache, image_lists, cited_count, image_slot):
    home = (KVH, LINE, ROWS + 1, HD)
    along_z = (NZ, GROUP + 1, HD)
    return pl.pallas_call(
        kernel,
        name="attend",
        out_shape=pltpu.VMEM((2, GROUP // 2 * HD), jnp.float32),
        in_specs=[pl.BlockSpec(memory_space=pl.ANY)] * 5,
        out_specs=pl.BlockSpec(memory_space=pltpu.VMEM),
        scratch_shapes=[
            pltpu.VMEM(queries.shape, jnp.bfloat16),
            pltpu.VMEM(image_cache.shape, jnp.bfloat16),
            pltpu.SMEM((LISTS, REQS), jnp.int32),
            pltpu.SMEM((REQS,), jnp.int32),
            pltpu.SMEM((IMAGES,), jnp.int32),
            pltpu.VMEM((KVH, ROWS, HD), jnp.bfloat16),
            pltpu.VMEM((LINE, KVH, ROWS, HD), jnp.bfloat16),
            pltpu.VMEM((KVH, SIDE, 2, TOK, HD), jnp.bfloat16),
            pltpu.VMEM((LINE, ROWS, SIDE * TOK), jnp.float32),
            pltpu.VMEM(home, jnp.float32),
            pltpu.VMEM(home, jnp.float32),
            pltpu.VMEM(along_z, jnp.float32),
            pltpu.VMEM(along_z, jnp.float32),
            pltpu.SemaphoreType.DMA((5,)),
            pltpu.SemaphoreType.DMA((2,)),
            pltpu.SemaphoreType.DMA((2,)),
            pltpu.SemaphoreType.DMA((KVH + 1,)),
            pltpu.SemaphoreType.DMA((KVH + 1,)),
            pltpu.SemaphoreType.DMA((KVH,)),
            pltpu.SemaphoreType.DMA((KVH,)),
            pltpu.SemaphoreType.DMA,
            pltpu.SemaphoreType.DMA,
            pltpu.SemaphoreType.REGULAR((4,)),
        ],
        compiler_params=pltpu.CompilerParams(
            collective_id=0, has_side_effects=True, vmem_limit_bytes=60 * 2**20
        ),
    )(queries, image_cache, image_lists.T, cited_count, image_slot)


def solution(mesh):
    return jax.shard_map(
        per_device,
        mesh=mesh,
        in_specs=(P("req", None), P("req", "tp", None), P(), P(), P()),
        out_specs=P("req", "tp"),
        check_vma=False,
    )
```

```python
import math

import jax
import jax.numpy as jnp
from jax import lax
from jax.experimental import pallas as pl
from jax.experimental.pallas import tpu as pltpu
from jax.sharding import PartitionSpec as P

KVH = 8
GROUP = 8
HD = 128
IMG_TOK = 1601
LISTS = 4
SIDE = 4
NZ = 16
REQS = 64
IMAGES = 32
TOK = 104
LINE = 2 * SIDE
ROWS = 16
STAGES = (0, 1, 2, 3, 6, 7, 4, 5)
NEG = -1e30
SCALE = math.log2(math.e) / math.sqrt(HD)
MESH = pl.DeviceIdType.MESH
FIRST_LATE = NZ // 2
GREETED = tuple(min(n, 8) if n < 12 else 7 if n == 12 else 6 for n in range(NZ))


def wait_bytes(ref, sem):
    pltpu.make_async_copy(ref, ref, sem).wait()


def kernel(
    q_hbm, cache_hbm, lists_hbm, count_hbm, slot_hbm, out_ref,
    q_ref, cache_ref, lists_ref, count_ref, slot_ref,
    q_own, q_buf, kv_buf, bias, home_out, home_in, z_out, z_in,
    own_sem, q_send, q_recv, kv_send, kv_recv, h_send, h_recv, z_send, z_recv, z_met,
):
    req = lax.axis_index("req")
    z = lax.axis_index("tp")
    core = lax.rem(req, 2)
    x = lax.div(req, 2 * SIDE)
    y = lax.rem(lax.div(req, 2), SIDE)
    even = core == 0

    def device(x_, y_, c_, z_=z):
        return ((x_ * SIDE + y_) * 2 + c_, z_)

    def along_x(d, c_):
        return device(lax.rem(x + d, SIDE), y, c_)

    def along_y(d, c_):
        return device(x, lax.rem(y + d, SIDE), c_)

    def along_z(d):
        return device(x, y, core, lax.rem(z + d + NZ, NZ))

    other_core = device(x, y, 1 - core)
    kv_place = jnp.where(even, x, y)
    q_place = jnp.where(even, y, x)

    barrier = pltpu.get_barrier_semaphore()
    met = [line(d, c_) for d in (2, 1, 3) for line in (along_x, along_y) for c_ in range(2)]
    met += [other_core]
    for there in met:
        pl.semaphore_signal(barrier, inc=1, device_id=there, device_id_type=MESH)
    own = [
        pltpu.make_async_copy(src, dst, own_sem.at[i])
        for i, (src, dst) in enumerate(
            (
                (q_hbm, q_ref),
                (cache_hbm, cache_ref),
                (lists_hbm, lists_ref),
                (count_hbm, count_ref),
                (slot_hbm, slot_ref),
            )
        )
    ]
    for copy in own:
        copy.start()

    late = z >= FIRST_LATE

    def near(d):
        return late & (z + d >= FIRST_LATE) & (z + d < NZ)

    for d in (-2, -1, 1, 2):

        @pl.when(near(d))
        def _():
            pl.semaphore_signal(barrier, inc=1, device_id=along_z(d), device_id_type=MESH)

    for n in range(NZ - 1, 0, -1):

        @pl.when(z < GREETED[n])
        def _():
            there = device(x, y, core, n)
            pl.semaphore_signal(barrier, inc=1, device_id=there, device_id_type=MESH)

    own[0].wait()
    for s, head in enumerate(STAGES):
        first = head * GROUP * HD
        mine = q_ref[:, first : first + GROUP * HD].astype(jnp.float32)
        rows = [mine[r : r + 1, g * HD : (g + 1) * HD] for r in range(2) for g in range(GROUP)]
        q_own[s] = jnp.concatenate(rows, axis=0).astype(jnp.bfloat16)
    q_buf[2 * q_place + core] = q_own[...]

    own[1].wait()
    for s, head in enumerate(STAGES):
        for i in range(2):
            first = (i * KVH + head) * HD
            kv_buf[s, kv_place, i] = cache_ref[0, :, first : first + HD]

    greeted = jnp.int32(len(met))
    for d in (-2, -1, 1, 2):
        greeted = greeted + jnp.where(near(d), 1, 0)
    for n in range(1, NZ):
        greeted = greeted + jnp.where(z == n, GREETED[n], 0)
    pl.semaphore_wait(barrier, greeted)

    def send(src, dst, sems, n, there):
        send_sem, recv_sem = sems
        pltpu.make_async_remote_copy(
            src_ref=src, dst_ref=dst, send_sem=send_sem.at[n], recv_sem=recv_sem.at[n],
            device_id=there, device_id_type=MESH,
        ).start()


    def send_kv(n, s, part):
        for d in (2, 1, 3):
            place = lax.rem(kv_place + d, SIDE)
            there = device(jnp.where(even, place, x), jnp.where(even, y, place), core)
            block = kv_buf.at[s, kv_place, part]
            send(block, block, (kv_send, kv_recv), n, there)

    def send_q(n, stages):
        for d in (2, 1, 3):
            for c, line, place in ((0, along_y, y), (1, along_x, x)):
                src, dst = q_own.at[stages], q_buf.at[2 * place + core, stages]
                send(src, dst, (q_send, q_recv), n, line(d, c))
        src, dst = q_own.at[stages], q_buf.at[2 * kv_place + core, stages]
        send(src, dst, (q_send, q_recv), n, other_core)

    both = slice(None)
    soon, later = pl.ds(0, 1), pl.ds(1, KVH - 1)
    send_q(0, soon)
    send_kv(0, 0, 0)
    send_kv(1, 0, 1)
    send_kv(2, 1, both)
    send_q(1, later)
    send_kv(3, 2, both)
    send_kv(4, 3, both)

    def tell(n, there):
        pl.semaphore_signal(z_met.at[n], inc=1, device_id=device(x, y, core, there), device_id_type=MESH)

    def pass_on(n, step):
        for d in (-step, step):

            @pl.when(near(d))
            def _():
                tell(n, z + d)

    def told(n, step):
        count = jnp.where(near(-step), 1, 0) + jnp.where(near(step), 1, 0)

        @pl.when(late & (count > 0))
        def _():
            pl.semaphore_wait(z_met.at[n], count)

    pass_on(0, 2)
    for n in range(FIRST_LATE - 1):

        @pl.when((n < z) & (z < FIRST_LATE))
        def _():
            tell(3, n)

    for copy in own[2:]:
        copy.wait()
    lanes = lax.broadcasted_iota(jnp.int32, (GROUP, SIDE * TOK), 1)
    image = sum(jnp.where(lanes >= m * TOK, 1, 0) for m in range(1, SIDE))
    valid = jnp.where(z * TOK + lanes - image * TOK < IMG_TOK, 0.0, NEG)
    first_slot = jnp.where(even, 2 * y, 2 * SIDE * x + 1)
    step = jnp.where(even, 2 * SIDE, 2)

    @pl.loop(0, LINE)
    def _(n):
        place = lax.div(n, 2)
        chip = jnp.where(even, x * SIDE + place, place * SIDE + y)
        for r in range(2):
            request = 4 * chip + 2 * lax.rem(n, 2) + r
            cited = count_ref[request]
            named = [jnp.where(j < cited, slot_ref[lists_ref[j, request]], -1) for j in range(LISTS)]
            level = valid
            for m in range(SIDE):
                slot = first_slot + step * m
                hit = jnp.int32(0)
                for name in named:
                    hit = hit + jnp.where(name == slot, 1, 0)
                level = level + jnp.where(image == m, jnp.where(hit > 0, 0.0, NEG), 0.0)
            bias[n, r * GROUP : (r + 1) * GROUP, :] = level

    told(0, 2)
    pass_on(1, 4)

    others, line_others = pl.ds(0, LINE - 1), pl.ds(0, SIDE - 1)
    iota = [lax.broadcasted_iota(jnp.int32, (1, 2, GROUP, HD), i) for i in range(4)]
    in_row = iota[3] == iota[1] * GROUP + iota[2]

    def work(s):
        if s == 0:
            wait_bytes(q_buf.at[others, soon], q_recv.at[0])
            wait_bytes(kv_buf.at[0, line_others, 0], kv_recv.at[0])
        else:
            if s == 1:
                wait_bytes(q_buf.at[others, later], q_recv.at[1])
            wait_bytes(kv_buf.at[s, line_others], kv_recv.at[s + 1])
        queries = q_buf[:, s].reshape(LINE * ROWS, HD)
        keys = kv_buf[s, :, 0].reshape(SIDE * TOK, HD)
        scores = lax.dot_general(
            queries, keys, (((1,), (1,)), ((), ())), preferred_element_type=jnp.float32
        )
        scores = scores * SCALE + bias[...].reshape(LINE * ROWS, SIDE * TOK)
        peak = jnp.max(scores, axis=1, keepdims=True)
        weights = jnp.exp2(scores - peak)
        total = jnp.sum(weights, axis=1, keepdims=True)
        high = weights.astype(jnp.bfloat16)
        low = (weights - high.astype(jnp.float32)).astype(jnp.bfloat16)
        if s == 0:
            wait_bytes(kv_buf.at[0, line_others, 1], kv_recv.at[1])
        values = kv_buf[s, :, 1].reshape(SIDE * TOK, HD)
        weighted = jnp.dot(high, values, preferred_element_type=jnp.float32)
        weighted += jnp.dot(low, values, preferred_element_type=jnp.float32)
        home_out[s, :, :ROWS, :] = (weighted / total).reshape(LINE, ROWS, HD)
        size = (peak + jnp.log2(total)).reshape(LINE, 2, GROUP, 1)
        row = jnp.sum(jnp.where(in_row, size, 0.0), axis=2, keepdims=True)
        home_out[s, :, ROWS:, :] = jnp.sum(row, axis=1)
        place = SIDE * core + q_place
        for d in (2, 1, 3):
            there = lax.rem(q_place + d, SIDE)
            for c in range(2):
                to = device(jnp.where(even, x, there), jnp.where(even, there, y), c)
                send(home_out.at[s, 2 * there + c], home_in.at[s, place], (h_send, h_recv), s, to)
        send(home_out.at[s, 2 * q_place + 1 - core], home_in.at[s, place], (h_send, h_recv), s, other_core)
        home_in[s, place] = home_out[s, 2 * q_place + core]

    diagonal = lax.broadcasted_iota(jnp.int32, (GROUP, HD), 0) == lax.broadcasted_iota(jnp.int32, (GROUP, HD), 1)
    low_rows = lax.broadcasted_iota(jnp.int32, (GROUP, HD), 0) < GROUP // 2

    def spread(s):
        wait_bytes(home_in.at[s, others], h_recv.at[s])
        row = home_in[s, :, ROWS:, :].reshape(LINE, 1, 1, HD)
        sizes = jnp.sum(jnp.where(in_row, row, 0.0), axis=3, keepdims=True)
        largest = jnp.max(sizes, axis=0)
        share = jnp.exp2(sizes - largest[None])
        total = jnp.sum(share, axis=0)
        share = share / total[None]
        size = largest + jnp.log2(total)
        results, logs = [], []
        for r in range(2):
            part = home_in[s, :, r * GROUP : (r + 1) * GROUP, :]
            results.append(jnp.sum(part * share[:, r], axis=0))
            logs.append(jnp.broadcast_to(size[r], (GROUP, HD)))
        for h in range(2):
            there = 2 * STAGES[s] + h
            tiles = []
            for a, b in (results, logs):
                if h == 0:
                    tiles.append(jnp.where(low_rows, a, pltpu.roll(b, GROUP // 2, 0)))
                else:
                    tiles.append(jnp.where(low_rows, pltpu.roll(a, GROUP // 2, 0), b))
            z_out[there, :GROUP, :] = tiles[0]
            z_out[there, GROUP:, :] = jnp.sum(jnp.where(diagonal, tiles[1], 0.0), axis=0, keepdims=True)

            @pl.when(z != there)
            def _():
                pltpu.make_async_remote_copy(
                    src_ref=z_out.at[there], dst_ref=z_in.at[z], send_sem=z_send, recv_sem=z_recv,
                    device_id=device(x, y, core, there), device_id_type=MESH,
                ).start()

            @pl.when(z == there)
            def _():
                z_in[z] = z_out[there]

    work(0)
    send_kv(5, 4, both)
    work(1)
    send_kv(6, 5, both)
    told(1, 4)
    for n in range(FIRST_LATE):

        @pl.when(late)
        def _():
            tell(2, n)

    work(2)
    send_kv(7, 6, both)
    @pl.when(z < FIRST_LATE - 1)
    def _():
        pl.semaphore_wait(z_met.at[3], FIRST_LATE - 1 - z)

    spread(0)
    work(3)
    send_kv(8, 7, both)
    spread(1)
    work(4)
    spread(2)
    work(5)
    spread(3)
    work(6)
    work(7)
    @pl.when(z < FIRST_LATE)
    def _():
        pl.semaphore_wait(z_met.at[2], NZ - FIRST_LATE)

    spread(4)
    spread(5)
    spread(6)
    spread(7)

    wait_bytes(q_buf.at[others, soon], q_send.at[0])
    wait_bytes(q_buf.at[others, later], q_send.at[1])
    for i in range(2):
        wait_bytes(kv_buf.at[0, line_others, i], kv_send.at[i])
    for s in range(1, KVH):
        wait_bytes(kv_buf.at[s, line_others], kv_send.at[s + 1])
    for s in range(KVH):
        wait_bytes(home_in.at[s, others], h_send.at[s])

    wait_bytes(z_in.at[pl.ds(0, NZ - 1)], z_recv)
    sizes = jnp.sum(jnp.where(diagonal[None], z_in[:, GROUP:, :], 0.0), axis=2, keepdims=True)
    largest = jnp.max(sizes, axis=0)
    share = jnp.exp2(sizes - largest[None])
    result = jnp.sum(z_in[:, :GROUP, :] * share, axis=0) / jnp.sum(share, axis=0)
    for r in range(2):
        for g in range(GROUP // 2):
            at = r * (GROUP // 2) + g
            out_ref[r : r + 1, g * HD : (g + 1) * HD] = result[at : at + 1]

    wait_bytes(z_in.at[pl.ds(0, NZ - 1)], z_send)


def per_device(queries, image_cache, image_lists, cited_count, image_slot):
    home = (KVH, LINE, ROWS + 1, HD)
    along_z = (NZ, GROUP + 1, HD)
    return pl.pallas_call(
        kernel,
        name="attend",
        out_shape=pltpu.VMEM((2, GROUP // 2 * HD), jnp.float32),
        in_specs=[pl.BlockSpec(memory_space=pl.ANY)] * 5,
        out_specs=pl.BlockSpec(memory_space=pltpu.VMEM),
        scratch_shapes=[
            pltpu.VMEM(queries.shape, jnp.bfloat16),
            pltpu.VMEM(image_cache.shape, jnp.bfloat16),
            pltpu.SMEM((LISTS, REQS), jnp.int32),
            pltpu.SMEM((REQS,), jnp.int32),
            pltpu.SMEM((IMAGES,), jnp.int32),
            pltpu.VMEM((KVH, ROWS, HD), jnp.bfloat16),
            pltpu.VMEM((LINE, KVH, ROWS, HD), jnp.bfloat16),
            pltpu.VMEM((KVH, SIDE, 2, TOK, HD), jnp.bfloat16),
            pltpu.VMEM((LINE, ROWS, SIDE * TOK), jnp.float32),
            pltpu.VMEM(home, jnp.float32),
            pltpu.VMEM(home, jnp.float32),
            pltpu.VMEM(along_z, jnp.float32),
            pltpu.VMEM(along_z, jnp.float32),
            pltpu.SemaphoreType.DMA((5,)),
            pltpu.SemaphoreType.DMA((2,)),
            pltpu.SemaphoreType.DMA((2,)),
            pltpu.SemaphoreType.DMA((KVH + 1,)),
            pltpu.SemaphoreType.DMA((KVH + 1,)),
            pltpu.SemaphoreType.DMA((KVH,)),
            pltpu.SemaphoreType.DMA((KVH,)),
            pltpu.SemaphoreType.DMA,
            pltpu.SemaphoreType.DMA,
            pltpu.SemaphoreType.REGULAR((4,)),
        ],
        compiler_params=pltpu.CompilerParams(
            collective_id=0, has_side_effects=True, vmem_limit_bytes=60 * 2**20
        ),
    )(queries, image_cache, image_lists.T, cited_count, image_slot)


def solution(mesh):
    return jax.shard_map(
        per_device,
        mesh=mesh,
        in_specs=(P("req", None), P("req", "tp", None), P(), P(), P()),
        out_specs=P("req", "tp"),
        check_vma=False,
    )
```

```python
import math

import jax
import jax.numpy as jnp
from jax import lax
from jax.experimental import pallas as pl
from jax.experimental.pallas import tpu as pltpu
from jax.sharding import PartitionSpec as P

KVH = 8
GROUP = 8
HD = 128
IMG_TOK = 1601
LISTS = 4
SIDE = 4
NZ = 16
REQS = 64
IMAGES = 32
TOK = 104
LINE = 2 * SIDE
ROWS = 16
STAGES = (0, 1, 2, 3, 6, 7, 4, 5)
NEG = -1e30
SCALE = math.log2(math.e) / math.sqrt(HD)
MESH = pl.DeviceIdType.MESH
FIRST_LATE = NZ // 2
GREETED = tuple(min(n, 8) if n < 12 else 7 if n == 12 else 6 for n in range(NZ))


def wait_bytes(ref, sem):
    pltpu.make_async_copy(ref, ref, sem).wait()


def kernel(
    q_hbm, cache_hbm, lists_hbm, count_hbm, slot_hbm, out_ref,
    q_ref, cache_ref, lists_ref, count_ref, slot_ref,
    q_own, q_buf, kv_buf, bias, home_out, home_in, z_out, z_in,
    own_sem, q_send, q_recv, kv_send, kv_recv, h_send, h_recv, z_send, z_recv, z_met,
):
    req = lax.axis_index("req")
    z = lax.axis_index("tp")
    core = lax.rem(req, 2)
    x = lax.div(req, 2 * SIDE)
    y = lax.rem(lax.div(req, 2), SIDE)
    even = core == 0

    def device(x_, y_, c_, z_=z):
        return ((x_ * SIDE + y_) * 2 + c_, z_)

    def along_x(d, c_):
        return device(lax.rem(x + d, SIDE), y, c_)

    def along_y(d, c_):
        return device(x, lax.rem(y + d, SIDE), c_)

    def along_z(d):
        return device(x, y, core, lax.rem(z + d + NZ, NZ))

    other_core = device(x, y, 1 - core)
    kv_place = jnp.where(even, x, y)
    q_place = jnp.where(even, y, x)

    barrier = pltpu.get_barrier_semaphore()
    met = [line(d, c_) for d in (2, 1, 3) for line in (along_x, along_y) for c_ in range(2)]
    met += [other_core]
    for there in met:
        pl.semaphore_signal(barrier, inc=1, device_id=there, device_id_type=MESH)
    own = [
        pltpu.make_async_copy(src, dst, own_sem.at[i])
        for i, (src, dst) in enumerate(
            (
                (q_hbm, q_ref),
                (cache_hbm, cache_ref),
                (lists_hbm, lists_ref),
                (count_hbm, count_ref),
                (slot_hbm, slot_ref),
            )
        )
    ]
    for copy in own:
        copy.start()

    late = z >= FIRST_LATE

    def near(d):
        return late & (z + d >= FIRST_LATE) & (z + d < NZ)

    for d in (-2, -1, 1, 2):

        @pl.when(near(d))
        def _():
            pl.semaphore_signal(barrier, inc=1, device_id=along_z(d), device_id_type=MESH)

    for n in range(NZ - 1, 0, -1):

        @pl.when(z < GREETED[n])
        def _():
            there = device(x, y, core, n)
            pl.semaphore_signal(barrier, inc=1, device_id=there, device_id_type=MESH)

    own[0].wait()
    for s, head in enumerate(STAGES):
        first = head * GROUP * HD
        mine = q_ref[:, first : first + GROUP * HD].astype(jnp.float32)
        rows = [mine[r : r + 1, g * HD : (g + 1) * HD] for r in range(2) for g in range(GROUP)]
        q_own[s] = jnp.concatenate(rows, axis=0).astype(jnp.bfloat16)
    q_buf[2 * q_place + core] = q_own[...]

    own[1].wait()
    for s, head in enumerate(STAGES):
        for i in range(2):
            first = (i * KVH + head) * HD
            kv_buf[s, kv_place, i] = cache_ref[0, :, first : first + HD]

    greeted = jnp.int32(len(met))
    for d in (-2, -1, 1, 2):
        greeted = greeted + jnp.where(near(d), 1, 0)
    for n in range(1, NZ):
        greeted = greeted + jnp.where(z == n, GREETED[n], 0)
    pl.semaphore_wait(barrier, greeted)

    def send(src, dst, sems, n, there):
        send_sem, recv_sem = sems
        pltpu.make_async_remote_copy(
            src_ref=src, dst_ref=dst, send_sem=send_sem.at[n], recv_sem=recv_sem.at[n],
            device_id=there, device_id_type=MESH,
        ).start()


    def send_kv(n, s, part):
        for d in (2, 1, 3):
            place = lax.rem(kv_place + d, SIDE)
            there = device(jnp.where(even, place, x), jnp.where(even, y, place), core)
            block = kv_buf.at[s, kv_place, part]
            send(block, block, (kv_send, kv_recv), n, there)

    def send_q(n, stages):
        for d in (2, 1, 3):
            for c, line, place in ((0, along_y, y), (1, along_x, x)):
                src, dst = q_own.at[stages], q_buf.at[2 * place + core, stages]
                send(src, dst, (q_send, q_recv), n, line(d, c))
        src, dst = q_own.at[stages], q_buf.at[2 * kv_place + core, stages]
        send(src, dst, (q_send, q_recv), n, other_core)

    both = slice(None)
    soon, second, later = pl.ds(0, 1), pl.ds(1, 1), pl.ds(2, KVH - 2)
    send_q(0, soon)
    send_kv(0, 0, 0)
    send_kv(1, 0, 1)
    send_q(1, second)
    send_kv(2, 1, both)
    send_q(2, later)
    send_kv(3, 2, both)
    send_kv(4, 3, both)

    def tell(n, there):
        pl.semaphore_signal(z_met.at[n], inc=1, device_id=device(x, y, core, there), device_id_type=MESH)

    def pass_on(n, step):
        for d in (-step, step):

            @pl.when(near(d))
            def _():
                tell(n, z + d)

    def told(n, step):
        count = jnp.where(near(-step), 1, 0) + jnp.where(near(step), 1, 0)

        @pl.when(late & (count > 0))
        def _():
            pl.semaphore_wait(z_met.at[n], count)

    pass_on(0, 2)
    for n in range(FIRST_LATE - 1):

        @pl.when((n < z) & (z < FIRST_LATE))
        def _():
            tell(3, n)

    for copy in own[2:]:
        copy.wait()
    lanes = lax.broadcasted_iota(jnp.int32, (GROUP, SIDE * TOK), 1)
    image = sum(jnp.where(lanes >= m * TOK, 1, 0) for m in range(1, SIDE))
    valid = jnp.where(z * TOK + lanes - image * TOK < IMG_TOK, 0.0, NEG)
    first_slot = jnp.where(even, 2 * y, 2 * SIDE * x + 1)
    step = jnp.where(even, 2 * SIDE, 2)

    @pl.loop(0, LINE)
    def _(n):
        place = lax.div(n, 2)
        chip = jnp.where(even, x * SIDE + place, place * SIDE + y)
        for r in range(2):
            request = 4 * chip + 2 * lax.rem(n, 2) + r
            cited = count_ref[request]
            named = [jnp.where(j < cited, slot_ref[lists_ref[j, request]], -1) for j in range(LISTS)]
            level = valid
            for m in range(SIDE):
                slot = first_slot + step * m
                hit = jnp.int32(0)
                for name in named:
                    hit = hit + jnp.where(name == slot, 1, 0)
                level = level + jnp.where(image == m, jnp.where(hit > 0, 0.0, NEG), 0.0)
            bias[n, r * GROUP : (r + 1) * GROUP, :] = level

    told(0, 2)
    pass_on(1, 4)

    others, line_others = pl.ds(0, LINE - 1), pl.ds(0, SIDE - 1)
    iota = [lax.broadcasted_iota(jnp.int32, (1, 2, GROUP, HD), i) for i in range(4)]
    in_row = iota[3] == iota[1] * GROUP + iota[2]

    def work(s):
        if s == 0:
            wait_bytes(q_buf.at[others, soon], q_recv.at[0])
            wait_bytes(kv_buf.at[0, line_others, 0], kv_recv.at[0])
        else:
            if s == 1:
                wait_bytes(q_buf.at[others, second], q_recv.at[1])
            if s == 2:
                wait_bytes(q_buf.at[others, later], q_recv.at[2])
            wait_bytes(kv_buf.at[s, line_others], kv_recv.at[s + 1])
        queries = q_buf[:, s].reshape(LINE * ROWS, HD)
        keys = kv_buf[s, :, 0].reshape(SIDE * TOK, HD)
        scores = lax.dot_general(
            queries, keys, (((1,), (1,)), ((), ())), preferred_element_type=jnp.float32
        )
        scores = scores * SCALE + bias[...].reshape(LINE * ROWS, SIDE * TOK)
        peak = jnp.max(scores, axis=1, keepdims=True)
        weights = jnp.exp2(scores - peak)
        total = jnp.sum(weights, axis=1, keepdims=True)
        high = weights.astype(jnp.bfloat16)
        low = (weights - high.astype(jnp.float32)).astype(jnp.bfloat16)
        if s == 0:
            wait_bytes(kv_buf.at[0, line_others, 1], kv_recv.at[1])
        values = kv_buf[s, :, 1].reshape(SIDE * TOK, HD)
        weighted = jnp.dot(high, values, preferred_element_type=jnp.float32)
        weighted += jnp.dot(low, values, preferred_element_type=jnp.float32)
        home_out[s, :, :ROWS, :] = (weighted / total).reshape(LINE, ROWS, HD)
        size = (peak + jnp.log2(total)).reshape(LINE, 2, GROUP, 1)
        row = jnp.sum(jnp.where(in_row, size, 0.0), axis=2, keepdims=True)
        home_out[s, :, ROWS:, :] = jnp.sum(row, axis=1)
        place = SIDE * core + q_place
        for d in (2, 1, 3):
            there = lax.rem(q_place + d, SIDE)
            for c in range(2):
                to = device(jnp.where(even, x, there), jnp.where(even, there, y), c)
                send(home_out.at[s, 2 * there + c], home_in.at[s, place], (h_send, h_recv), s, to)
        send(home_out.at[s, 2 * q_place + 1 - core], home_in.at[s, place], (h_send, h_recv), s, other_core)
        home_in[s, place] = home_out[s, 2 * q_place + core]

    diagonal = lax.broadcasted_iota(jnp.int32, (GROUP, HD), 0) == lax.broadcasted_iota(jnp.int32, (GROUP, HD), 1)
    low_rows = lax.broadcasted_iota(jnp.int32, (GROUP, HD), 0) < GROUP // 2

    def spread(s):
        wait_bytes(home_in.at[s, others], h_recv.at[s])
        row = home_in[s, :, ROWS:, :].reshape(LINE, 1, 1, HD)
        sizes = jnp.sum(jnp.where(in_row, row, 0.0), axis=3, keepdims=True)
        largest = jnp.max(sizes, axis=0)
        share = jnp.exp2(sizes - largest[None])
        total = jnp.sum(share, axis=0)
        share = share / total[None]
        size = largest + jnp.log2(total)
        results, logs = [], []
        for r in range(2):
            part = home_in[s, :, r * GROUP : (r + 1) * GROUP, :]
            results.append(jnp.sum(part * share[:, r], axis=0))
            logs.append(jnp.broadcast_to(size[r], (GROUP, HD)))
        for h in range(2):
            there = 2 * STAGES[s] + h
            tiles = []
            for a, b in (results, logs):
                if h == 0:
                    tiles.append(jnp.where(low_rows, a, pltpu.roll(b, GROUP // 2, 0)))
                else:
                    tiles.append(jnp.where(low_rows, pltpu.roll(a, GROUP // 2, 0), b))
            z_out[there, :GROUP, :] = tiles[0]
            z_out[there, GROUP:, :] = jnp.sum(jnp.where(diagonal, tiles[1], 0.0), axis=0, keepdims=True)

            @pl.when(z != there)
            def _():
                pltpu.make_async_remote_copy(
                    src_ref=z_out.at[there], dst_ref=z_in.at[z], send_sem=z_send, recv_sem=z_recv,
                    device_id=device(x, y, core, there), device_id_type=MESH,
                ).start()

            @pl.when(z == there)
            def _():
                z_in[z] = z_out[there]

    work(0)
    send_kv(5, 4, both)
    work(1)
    send_kv(6, 5, both)
    told(1, 4)
    for n in range(FIRST_LATE):

        @pl.when(late)
        def _():
            tell(2, n)

    work(2)
    send_kv(7, 6, both)
    @pl.when(z < FIRST_LATE - 1)
    def _():
        pl.semaphore_wait(z_met.at[3], FIRST_LATE - 1 - z)

    spread(0)
    work(3)
    send_kv(8, 7, both)
    spread(1)
    work(4)
    spread(2)
    work(5)
    spread(3)
    work(6)
    work(7)
    @pl.when(z < FIRST_LATE)
    def _():
        pl.semaphore_wait(z_met.at[2], NZ - FIRST_LATE)

    spread(4)
    spread(5)
    spread(6)
    spread(7)

    wait_bytes(q_buf.at[others, soon], q_send.at[0])
    wait_bytes(q_buf.at[others, second], q_send.at[1])
    wait_bytes(q_buf.at[others, later], q_send.at[2])
    for i in range(2):
        wait_bytes(kv_buf.at[0, line_others, i], kv_send.at[i])
    for s in range(1, KVH):
        wait_bytes(kv_buf.at[s, line_others], kv_send.at[s + 1])
    for s in range(KVH):
        wait_bytes(home_in.at[s, others], h_send.at[s])

    wait_bytes(z_in.at[pl.ds(0, NZ - 1)], z_recv)
    sizes = jnp.sum(jnp.where(diagonal[None], z_in[:, GROUP:, :], 0.0), axis=2, keepdims=True)
    largest = jnp.max(sizes, axis=0)
    share = jnp.exp2(sizes - largest[None])
    result = jnp.sum(z_in[:, :GROUP, :] * share, axis=0) / jnp.sum(share, axis=0)
    for r in range(2):
        for g in range(GROUP // 2):
            at = r * (GROUP // 2) + g
            out_ref[r : r + 1, g * HD : (g + 1) * HD] = result[at : at + 1]

    wait_bytes(z_in.at[pl.ds(0, NZ - 1)], z_send)


def per_device(queries, image_cache, image_lists, cited_count, image_slot):
    home = (KVH, LINE, ROWS + 1, HD)
    along_z = (NZ, GROUP + 1, HD)
    return pl.pallas_call(
        kernel,
        name="attend",
        out_shape=pltpu.VMEM((2, GROUP // 2 * HD), jnp.float32),
        in_specs=[pl.BlockSpec(memory_space=pl.ANY)] * 5,
        out_specs=pl.BlockSpec(memory_space=pltpu.VMEM),
        scratch_shapes=[
            pltpu.VMEM(queries.shape, jnp.bfloat16),
            pltpu.VMEM(image_cache.shape, jnp.bfloat16),
            pltpu.SMEM((LISTS, REQS), jnp.int32),
            pltpu.SMEM((REQS,), jnp.int32),
            pltpu.SMEM((IMAGES,), jnp.int32),
            pltpu.VMEM((KVH, ROWS, HD), jnp.bfloat16),
            pltpu.VMEM((LINE, KVH, ROWS, HD), jnp.bfloat16),
            pltpu.VMEM((KVH, SIDE, 2, TOK, HD), jnp.bfloat16),
            pltpu.VMEM((LINE, ROWS, SIDE * TOK), jnp.float32),
            pltpu.VMEM(home, jnp.float32),
            pltpu.VMEM(home, jnp.float32),
            pltpu.VMEM(along_z, jnp.float32),
            pltpu.VMEM(along_z, jnp.float32),
            pltpu.SemaphoreType.DMA((5,)),
            pltpu.SemaphoreType.DMA((3,)),
            pltpu.SemaphoreType.DMA((3,)),
            pltpu.SemaphoreType.DMA((KVH + 1,)),
            pltpu.SemaphoreType.DMA((KVH + 1,)),
            pltpu.SemaphoreType.DMA((KVH,)),
            pltpu.SemaphoreType.DMA((KVH,)),
            pltpu.SemaphoreType.DMA,
            pltpu.SemaphoreType.DMA,
            pltpu.SemaphoreType.REGULAR((4,)),
        ],
        compiler_params=pltpu.CompilerParams(
            collective_id=0, has_side_effects=True, vmem_limit_bytes=60 * 2**20
        ),
    )(queries, image_cache, image_lists.T, cited_count, image_slot)


def solution(mesh):
    return jax.shard_map(
        per_device,
        mesh=mesh,
        in_specs=(P("req", None), P("req", "tp", None), P(), P(), P()),
        out_specs=P("req", "tp"),
        check_vma=False,
    )
```
